128 devices in a mesh: row: 8 (over y, core), col: 16 (over z, x).
Axes of the slice: x: 4, y: 4, z: 4, core: 2. Of those that a mesh axis runs over, the one named last changes fastest.
Arguments:
- obs_jac: bfloat16 [4096, 2, 1024, 128], P(('row', 'col')), may hold values from -0.1265625 to 0.1265625
- rad_jac: float32 [4096, 2, 1024], P(('row', 'col')), may hold values from -4 to 4
- obs_residual: float32 [4096, 2, 1024], P(('row', 'col')), may hold values from -6 to 6
- track_damping: float32 [4096, 1024], P(('row', 'col')), may hold values from 0.2 to 5
- track_block_column: int32 [4096, 1], P(('row', 'col')), may hold values from 0 to 15; in each aligned block of 32 rows (0 to 31, 32 to 63, ...) at most 3 rows name the same one
- track_slot: int32 [4096], P(('row', 'col')), may hold values from 0 to 31
- pair_rows: int32 [4096], P(('row', 'col')), may hold values from 0 to 255
- pair_cols: int32 [4096], P(('row', 'col')), may hold values from 0 to 127
- image_damping: float32 [2048, 128], P(('row', 'col')), may hold values from 0.1 to 2
Outputs:
- update: float32 [2048, 128], P(('row', 'col'))
- residual: float32 [2048, 128], P(('row', 'col'))
The draws below stay inside these ranges and needn't reach their ends.
Inputs may be any that keep to these rules, and one draw needn't show every extreme that they name: `track_block_column`: among the track blocks of one device, at most 3 name the same block column; some device has exactly 3 for some column.
All inputs are finite; a program needn't handle non-finite values.
Results may differ from the reference program's by a relative error of at most 0.02.
Values may be sent and summed in bfloat16 or wider, within the bound.
A program may use at most 192 MiB of HBM per device.

```python
import math
import jax
import jax.numpy as jnp
import numpy as np
from jax import lax

P_SIZE = 128
TB = 1024
TBLK_DEV = 32
PAIRS_DEV = 32
IMG_DEV = 16
ITERS = 3
CAP = 3
IMG_ROW = 256
IMG_COL = 128
NI = 2048
NB = 4096
NP = 4096
N_ROW = 8
N_COL = 16


def row_fraction(count, per_row):
    owner = jnp.arange(count, dtype=jnp.int32) // per_row
    return owner.astype(jnp.float32) / float(max(N_ROW - 1, 1))


def draw_obs_jac(key, part):
    key = jax.random.fold_in(key, 11)
    fractions = row_fraction(NB, TBLK_DEV * N_COL)

    def one_block(pieces):
        index, fraction = pieces
        block_key = jax.random.fold_in(key, index)
        first_key, second_key = jax.random.split(block_key)
        coupling = 0.85 * fraction
        first = jax.random.truncated_normal(first_key, -4.0, 4.0, (TB, P_SIZE), jnp.float32)
        second = jax.random.truncated_normal(second_key, -4.0, 4.0, (TB, P_SIZE), jnp.float32)
        mixed = jnp.clip(coupling * first + jnp.sqrt(1.0 - coupling * coupling) * second, -4.0, 4.0)
        scale = float(TB) ** (-0.5)
        return (jnp.stack([first, mixed], axis=0) * scale).astype(jnp.bfloat16)
    return lax.map(one_block, (jnp.arange(NB, dtype=jnp.int32), fractions))


def draw_rad_jac(key, part):
    key = jax.random.fold_in(key, 23)
    first_key, second_key = jax.random.split(key)
    coupling = (0.9 * row_fraction(NB, TBLK_DEV * N_COL))[:, None]
    first = jax.random.truncated_normal(first_key, -4.0, 4.0, (NB, TB), jnp.float32)
    second = jax.random.truncated_normal(second_key, -4.0, 4.0, (NB, TB), jnp.float32)
    mixed = jnp.clip(coupling * first + jnp.sqrt(1.0 - coupling * coupling) * second, -4.0, 4.0)
    return jnp.stack([first, mixed], axis=1)


def draw_image_damping(key, part):
    key = jax.random.fold_in(key, 37)
    fractions = row_fraction(NI, IMG_ROW)[:, None]
    spread = jax.random.uniform(key, (NI, P_SIZE), jnp.float32)
    exponent = (1.0 - fractions) * 0.6 + 0.4 * spread
    return jnp.clip(0.1 * jnp.exp(exponent * math.log(20.0)), 0.1, 2.0)


def plant(values, own_key, least, largest):
    index_at = [jax.random.randint(jax.random.fold_in(own_key, axis), (), 0, length) for axis, length in enumerate(values.shape)]
    main_axis = values.shape.index(max(values.shape))
    beside = index_at[:main_axis] + [(index_at[main_axis] + 1) % values.shape[main_axis]] + index_at[main_axis + 1:]
    return values.at[tuple(index_at)].set(least).at[tuple(beside)].set(largest)


def shard_levels(rng, shape, cuts, low, largest):
    factor_of = 1.0
    for position, shards_of in cuts:
        draws = jax.random.uniform(jax.random.fold_in(jax.random.fold_in(rng, 6), position), (shards_of,), jnp.float32, low / len(cuts), largest / len(cuts))
        factor_of = factor_of * jnp.repeat(jnp.exp(draws), shape[position] // shards_of).reshape((-1,) + (1,) * (len(shape) - 1 - position))
    return factor_of


def shared_out(stream_key, own, number, rows, number_of, top, most, lean):
    order = jax.random.permutation(stream_key, number_of)
    heavy_load, common = portions_of(number_of, rows * top, most, lean, True), portions_of(number_of, rows * top, most, lean, False)
    places = jnp.arange(number_of)

    def named(tallies, offset_by):
        used = int((tallies > 0).sum())
        fixed = max(1, used // 4)
        passed = fixed + (places - fixed + offset_by * (used - fixed)) % max(1, number_of - fixed)
        return jnp.zeros((number_of,), jnp.int32).at[order[jnp.where(places < fixed, places, passed)]].set(jnp.asarray(tallies, jnp.int32))

    tallies = jnp.where(number % 4 == 0, named(heavy_load, number // 4), named(common, number - number // 4 - 1))
    mixed = jax.random.permutation(jax.random.fold_in(own, 3), number_of)
    source_of, sink = mixed[0:number_of // 2 * 2:2], mixed[1:number_of // 2 * 2:2]
    margin = jnp.minimum(tallies[source_of] - 1, most - tallies[sink]) // 2
    margin = jnp.where((source_of == order[0]) | (sink == order[0]) | (tallies[sink] == 0), 0, jnp.maximum(margin, 0))
    passed = jax.random.randint(jax.random.fold_in(own, 4), (number_of // 2,), 0, 1 << 20) % (margin + 1)
    tallies = tallies.at[source_of].add(-passed).at[sink].add(passed)
    items = jnp.searchsorted(jnp.cumsum(tallies), jnp.arange(rows * top), side="right").astype(jnp.int32)
    table = items.reshape(top, rows).T
    table = table[jax.random.permutation(jax.random.fold_in(own, 1), rows)]
    offset_by = jax.random.randint(jax.random.fold_in(own, 2), (rows, 1), 0, top)
    return jnp.take_along_axis(table, (jnp.arange(top)[None, :] + offset_by) % top, axis=1)


def portions_of(count, total, bound, lean, full):
    loads = [(1 << 20) // math.isqrt(rank ** lean) + 1 for rank in range(1, count + 1)]
    largest = bound if full else min(bound, max(-(-total // count), total * loads[0] // sum(loads)))
    least = 1 if total - largest >= count - 1 else 0
    given, surplus = [largest] + [least] * (count - 1), total - largest - least * (count - 1)
    while surplus > 0:
        free = [i for i in range(1, count) if given[i] < largest] or [i for i in range(1, count) if given[i] < bound]
        mass, budget = sum([loads[i] for i in free]), surplus
        for i in free:
            extra = min(bound - given[i], max(1, budget * loads[i] // mass), surplus)
            given[i] = given[i] + extra
            surplus = surplus - extra
    return np.array(given)


def bell_draw(rng, dims, width, limit, cuts=(), held_as=jnp.bfloat16):
    values = jax.random.normal(rng, dims, jnp.float32) * width
    if len(cuts) > 0:
        values = shard_levels(rng, dims, cuts, -0.22, 0.18) * values
    return jnp.clip(values, min=-limit, max=limit).astype(held_as)


def setup_inputs(seed: int = 0) -> dict:
    key_of = jax.random.split(jax.random.key(seed), 10)
    obs_jac = draw_obs_jac(jax.random.fold_in(key_of[9], 71), 0)
    rad_jac = draw_rad_jac(jax.random.fold_in(key_of[9], 71), 0)
    obs_residual = bell_draw(key_of[2], (NB, 2, TB), 1.0, 6.0, ((0, 128),), jnp.float32)
    track_damping = jnp.clip(jnp.exp(math.log(5.0) - 3.218876 * jax.random.uniform(key_of[3], (NB, TB), jnp.float32) ** shard_levels(key_of[3], (NB, TB), ((0, 128),), -0.2, 0.2)), 0.2, 5.0)
    track_block_column_keys = jax.random.split(jax.random.fold_in(key_of[4], 1), NB // TBLK_DEV)
    track_block_column_turns = jax.random.permutation(jax.random.fold_in(key_of[4], 3), NB // TBLK_DEV)
    track_block_column = jax.vmap(lambda own, number: shared_out(jax.random.fold_in(key_of[4], 2), own, number, TBLK_DEV, N_COL, 1, CAP, 2))(track_block_column_keys, track_block_column_turns).reshape((NB, 1))
    track_slot = plant(jax.random.randint(key_of[5], (NB,), 0, PAIRS_DEV), jax.random.fold_in(key_of[5], 1), 0, PAIRS_DEV - 1).astype(jnp.int32)
    pair_rows = plant(jax.random.randint(key_of[6], (NP,), 0, IMG_ROW), jax.random.fold_in(key_of[6], 1), 0, IMG_ROW - 1).astype(jnp.int32)
    pair_cols = plant(jax.random.randint(key_of[7], (NP,), 0, IMG_COL), jax.random.fold_in(key_of[7], 1), 0, IMG_COL - 1).astype(jnp.int32)
    image_damping = draw_image_damping(jax.random.fold_in(key_of[9], 71), 0)
    return {"obs_jac": obs_jac, "rad_jac": rad_jac, "obs_residual": obs_residual, "track_damping": track_damping, "track_block_column": track_block_column, "track_slot": track_slot, "pair_rows": pair_rows, "pair_cols": pair_cols, "image_damping": image_damping}


def coefficients(rad, resid, damp):
    first_h = rad[..., 0, :]
    second_h = rad[..., 1, :]
    first_e = resid[..., 0, :]
    second_e = resid[..., 1, :]
    total = first_h * first_h + second_h * second_h + damp
    track_grad = first_h * first_e + second_h * second_e
    track_coefficient = jnp.stack([1.0 - first_h * first_h / total, 1.0 - second_h * second_h / total,
                      -first_h * second_h / total, first_e - first_h * track_grad / total,
                      second_e - second_h * track_grad / total], axis=-2)
    return track_coefficient.astype(jnp.bfloat16)


def form_terms(jac, track_coefficient):
    first_image = jac[:, 0]
    second_image = jac[:, 1]
    right = jnp.stack([first_image, second_image, second_image], axis=1).astype(jnp.float32)
    weighted = (track_coefficient[:, :3, :, None].astype(jnp.float32) * right).astype(jnp.bfloat16)
    left = jnp.stack([first_image, second_image, first_image], axis=1)
    blocks = jnp.einsum('kjtp,kjtq->kjpq', left.astype(jnp.float32), weighted.astype(jnp.float32),
                        precision=lax.Precision.HIGHEST).astype(jnp.bfloat16)
    vectors = jnp.einsum('kjt,kjtp->kjp', track_coefficient[:, 3:].astype(jnp.float32), jac.astype(jnp.float32),
                         precision=lax.Precision.HIGHEST).astype(jnp.bfloat16)
    return blocks, vectors


def reference(obs_jac, rad_jac, obs_residual, track_damping, track_block_column, track_slot, pair_rows, pair_cols, image_damping):
    devices = N_ROW * N_COL
    npairs = PAIRS_DEV * devices
    nimages = IMG_DEV * devices
    highest = lax.Precision.HIGHEST
    block_ids = jnp.arange(TBLK_DEV * devices, dtype=jnp.int32)
    owner_row = (block_ids // TBLK_DEV) // N_COL
    pair_of_block = (owner_row * N_COL + track_block_column[:, 0]) * PAIRS_DEV + track_slot
    jac_dev = obs_jac.reshape(devices, TBLK_DEV, 2, TB, P_SIZE)
    rad_dev = rad_jac.reshape(devices, TBLK_DEV, 2, TB)
    res_dev = obs_residual.reshape(devices, TBLK_DEV, 2, TB)
    damp_dev = track_damping.reshape(devices, TBLK_DEV, TB)
    pair_shard_list = pair_of_block.reshape(devices, TBLK_DEV)

    def accumulate(carry, pieces):
        acc_blocks, acc_vectors = carry
        jac, rad, res, damp, target = pieces
        track_coefficient = coefficients(rad, res, damp)
        blocks, vectors = form_terms(jac, track_coefficient)
        acc_blocks = acc_blocks.at[target].add(blocks.astype(jnp.float32))
        acc_vectors = acc_vectors.at[target].add(vectors.astype(jnp.float32))
        return (acc_blocks, acc_vectors), None

    start = (jnp.zeros((npairs, 3, P_SIZE, P_SIZE), jnp.float32), jnp.zeros((npairs, 2, P_SIZE), jnp.float32))
    (pair_blocks, pair_vectors), _ = lax.scan(accumulate, start, (jac_dev, rad_dev, res_dev, damp_dev, pair_shard_list))

    pair_ids = jnp.arange(npairs, dtype=jnp.int32)
    device_of = pair_ids // PAIRS_DEV
    block_row = device_of // N_COL
    block_col = device_of % N_COL
    image_a = block_row * IMG_ROW + pair_rows
    image_b = (pair_cols // IMG_DEV) * IMG_ROW + block_col * IMG_DEV + pair_cols % IMG_DEV

    def operate(field):
        first_in = field[image_a]
        second_in = field[image_b]
        first_out = jnp.einsum('pab,pb->pa', pair_blocks[:, 0], first_in, precision=highest)
        first_out = first_out + jnp.einsum('pab,pb->pa', pair_blocks[:, 2], second_in, precision=highest)
        second_out = jnp.einsum('pab,pb->pa', pair_blocks[:, 1], second_in, precision=highest)
        second_out = second_out + jnp.einsum('pba,pb->pa', pair_blocks[:, 2], first_in, precision=highest)
        result = image_damping * field
        result = result + jax.ops.segment_sum(first_out, image_a, num_segments=nimages)
        return result + jax.ops.segment_sum(second_out, image_b, num_segments=nimages)

    right_side = jax.ops.segment_sum(pair_vectors[:, 0], image_a, num_segments=nimages)
    right_side = right_side + jax.ops.segment_sum(pair_vectors[:, 1], image_b, num_segments=nimages)
    first_diag = jnp.diagonal(pair_blocks[:, 0], axis1=1, axis2=2)
    second_diag = jnp.diagonal(pair_blocks[:, 1], axis1=1, axis2=2)
    diagonal = image_damping + jax.ops.segment_sum(first_diag, image_a, num_segments=nimages)
    diagonal = diagonal + jax.ops.segment_sum(second_diag, image_b, num_segments=nimages)

    update = jnp.zeros((nimages, P_SIZE), jnp.float32)
    residual = right_side
    scaled = residual / diagonal
    direction = scaled
    inner_now = jnp.sum(residual * scaled)
    for iteration in range(ITERS):
        image = operate(direction)
        step_length = inner_now / jnp.sum(direction * image)
        update = update + step_length * direction
        residual = residual - step_length * image
        scaled = residual / diagonal
        inner_next = jnp.sum(residual * scaled)
        direction = scaled + (inner_next / inner_now) * direction
        inner_now = inner_next
    return update, residual
```

```python
import jax
import jax.numpy as jnp
from jax import lax
from jax.experimental import pallas as pl
from jax.experimental.pallas import tpu as pltpu
from jax.sharding import PartitionSpec as P

ITERS = 3
N_ROW = 8
N_COL = 16
BLOCKS = 32
IMG = 16
IMG_ROW = N_COL * IMG
IMG_COL = N_ROW * IMG
LANES = 128
TRACKS = 1024
STEP = 2
CAP = 3
SLOT = 8
SENT = 4
SLOTS = N_COL * SLOT
PHASES = 3 + 1 + 6 * ITERS
MESH = pl.DeviceIdType.MESH
F32 = jnp.float32
BF16 = jnp.bfloat16


def dot(left, right):
    return jnp.dot(left, right, preferred_element_type=F32)


def halves(value):
    high = value.astype(BF16)
    low = (value - high.astype(F32)).astype(BF16)
    return high, low


def hot_dot(hot, value):
    both = dot(hot, jnp.concatenate(halves(value), axis=1))
    return both[:, 0:LANES] + both[:, LANES : 2 * LANES]


def iota(shape, axis):
    return lax.broadcasted_iota(jnp.int32, shape, axis).astype(F32)


def column_of(row_vector):
    n = row_vector.shape[1]
    return jnp.sum(
        jnp.where(iota((n, n), 0) == iota((n, n), 1), row_vector, 0.0), axis=1, keepdims=True
    )


def fold(value):
    return jnp.sum(value, axis=0, keepdims=True)


def total_of(value):
    return jnp.sum(value, axis=(0, 1), keepdims=True)


def spread_row(row):
    tile = jnp.broadcast_to(row, (16, TRACKS)).astype(BF16)
    return jnp.concatenate([tile] * 8, axis=0)


def block_terms(jac0, jac1, rad, resid, damp):
    h0, h1 = rad[0:1, :], rad[1:2, :]
    e0, e1 = resid[0:1, :], resid[1:2, :]
    inverse = 1.0 / (h0 * h0 + h1 * h1 + damp)
    grad = (h0 * e0 + h1 * e1) * inverse
    coef0 = spread_row(1.0 - h0 * h0 * inverse)
    coef1 = spread_row(1.0 - h1 * h1 * inverse)
    coef2 = spread_row(-h0 * h1 * inverse)
    coef3 = jnp.broadcast_to(e0 - h0 * grad, (16, TRACKS)).astype(BF16)
    coef4 = jnp.broadcast_to(e1 - h1 * grad, (16, TRACKS)).astype(BF16)
    jac0_t, jac1_t = jac0.T, jac1.T
    first = dot(jnp.concatenate([coef0 * jac0_t, coef3], axis=0), jac0)
    second = dot(jnp.concatenate([coef1 * jac1_t, coef4], axis=0), jac1)
    first, second = first.astype(BF16), second.astype(BF16)
    block_a, vector_a = first[0:128], first[128:144]
    block_b, vector_b = second[0:128], second[128:144]
    eye = iota((LANES, LANES), 0) == iota((LANES, LANES), 1)
    diag_a = fold(jnp.where(eye, block_a.astype(F32), 0.0))
    diag_b = fold(jnp.where(eye, block_b.astype(F32), 0.0))
    terms_a = jnp.concatenate([vector_a.astype(F32)[0:1], diag_a], axis=1)
    terms_b = jnp.concatenate([vector_b.astype(F32)[0:1], diag_b], axis=1)
    return block_a, block_b, coef2 * jac1_t, terms_a, terms_b


def kernel(
    jac_hbm,
    rad_hbm,
    resid_hbm,
    track_hbm,
    damp_ref,
    column_ref,
    slot_ref,
    rows_ref,
    cols_ref,
    state_ref,
    jac_ref,
    rad_ref,
    resid_ref,
    track_ref,
    weight_a,
    weight_b,
    weight_c,
    cross_ref,
    terms_a,
    terms_b,
    index_src,
    index_buf,
    rhs_b_src,
    rhs_b_buf,
    rhs_a_src,
    rhs_a_buf,
    rhs_r_src,
    rhs_r_buf,
    near_src,
    near_buf,
    field_src,
    field_buf,
    pick_src,
    pick_buf,
    prod_src,
    prod_buf,
    part_a_src,
    part_a_buf,
    part_b_src,
    part_b_buf,
    left_buf,
    load_sem,
    jac_sem,
    send_sem,
    recv_sem,
):
    row, col = lax.axis_index("row"), lax.axis_index("col")

    small = [
        pltpu.make_async_copy(src, dst, load_sem.at[i])
        for i, (src, dst) in enumerate(
            [(rad_hbm, rad_ref), (resid_hbm, resid_ref), (track_hbm, track_ref)]
        )
    ]
    for copy in small:
        copy.start()

    def load(step):
        part = pl.ds(step * STEP, STEP)
        return pltpu.make_async_copy(jac_hbm.at[part], jac_ref.at[part], jac_sem.at[step])

    def start_load(step, carry):
        load(step).start()
        return carry

    lax.fori_loop(0, BLOCKS // STEP, start_load, 0)

    for ref in (index_buf, rhs_b_buf, pick_buf, prod_buf):
        ref[...] = jnp.zeros_like(ref)

    barrier = pltpu.get_barrier_semaphore()

    col_hi, col_lo = lax.div(col, 4), lax.rem(col, 4)
    row_hi, row_lo = lax.div(row, 2), lax.rem(row, 2)
    col_steps = sorted(
        [(i, j) for i in range(4) for j in range(4) if i or j],
        key=lambda step: -sum(min(d, 4 - d) for d in step),
    )
    row_steps = [(i, j) for i in (2, 1, 3, 0) for j in (1, 0) if i or j]
    col_peers = [lax.rem(col_hi + i, 4) * 4 + lax.rem(col_lo + j, 4) for i, j in col_steps]
    row_peers = [lax.rem(row_hi + i, 4) * 2 + lax.rem(row_lo + j, 2) for i, j in row_steps]

    for peer in col_peers:
        pl.semaphore_signal(barrier, inc=1, device_id=(row, peer), device_id_type=MESH)
    for peer in row_peers:
        pl.semaphore_signal(barrier, inc=1, device_id=(peer, col), device_id_type=MESH)

    phases = iter(range(PHASES))
    pending = []

    def exchange(source, target, over_col, rows=None):
        phase = next(phases)
        peers, me = (col_peers, col) if over_col else (row_peers, row)
        rows = pl.ds(0, target.shape[1] if rows is None else rows)
        for peer in peers:
            pltpu.make_async_remote_copy(
                src_ref=source(peer).at[rows],
                dst_ref=target.at[me, rows],
                send_sem=send_sem.at[phase],
                recv_sem=recv_sem.at[phase],
                device_id=(row, peer) if over_col else (peer, col),
                device_id_type=MESH,
            ).start()
        whole = target.at[pl.ds(0, len(peers)), rows]
        copy = pltpu.make_async_remote_copy(
            src_ref=whole,
            dst_ref=whole,
            send_sem=send_sem.at[phase],
            recv_sem=recv_sem.at[phase],
            device_id=(row, peer) if over_col else (peer, col),
            device_id_type=MESH,
        )
        pending.append(copy)
        return copy

    def form(first, last):
        def one(step, carry):
            load(step).wait()
            for i in range(STEP):
                k = step * STEP + i
                block_a, block_b, cross, row_a, row_b = block_terms(
                    jac_ref[k, 0], jac_ref[k, 1], rad_ref[k], resid_ref[k], track_ref[pl.ds(k, 1), :]
                )
                at = pl.ds(pl.multiple_of(k * LANES, LANES), LANES)
                weight_a[at, 0:LANES] = block_a
                weight_b[at, :] = block_b
                cross_ref[k] = cross
                terms_a[pl.ds(k, 1), :] = row_a
                terms_b[pl.ds(k, 1), :] = row_b
            return carry

        lax.fori_loop(first // STEP, last // STEP, one, 0)

    def form_cross(first, last):
        def one(step, carry):
            for i in range(STEP):
                k = step * STEP + i
                at = pl.ds(pl.multiple_of(k * LANES, LANES), LANES)
                block_c = dot(cross_ref[k], jac_ref[k, 0]).astype(BF16)
                weight_c[at, :] = block_c
                weight_a[at, LANES : 2 * LANES] = block_c.T
            return carry

        lax.fori_loop(first // STEP, last // STEP, one, 0)

    for copy in small:
        copy.wait()
    form(0, 8)

    column_row = column_ref[...].astype(F32)
    slot_row = slot_ref[...].astype(F32)
    column = column_of(column_row)
    same = jnp.logical_and(
        column == column_row, iota((BLOCKS, BLOCKS), 1) < iota((BLOCKS, BLOCKS), 0)
    )
    place = jnp.sum(jnp.where(same, 1.0, 0.0), axis=1, keepdims=True)
    place_col = column * SLOT + place
    place_row = jnp.sum(
        jnp.where(iota((BLOCKS, BLOCKS), 0) == iota((BLOCKS, BLOCKS), 1), place_col, 0.0),
        axis=0,
        keepdims=True,
    )
    send_true = iota((SLOTS, BLOCKS), 0) == place_row
    send_hot = jnp.where(send_true, 1.0, 0.0).astype(BF16)
    take_hot = jnp.where(iota((BLOCKS, SLOTS), 1) == place_col, 1.0, 0.0).astype(BF16)
    slots_out = jnp.sum(jnp.where(send_true, slot_row + 1.0, 0.0), axis=1, keepdims=True) - 1.0
    index_src[...] = jnp.broadcast_to(slots_out, (SLOTS, LANES)).reshape(N_COL, SLOT, LANES)
    for j in range(N_COL):
        index_src[j, CAP : CAP + 1, 0:BLOCKS] = rows_ref[...].astype(F32)
    index_buf[col] = index_src[col]
    pl.semaphore_wait(barrier, N_COL + N_ROW - 2)
    copy = exchange(lambda peer: index_src.at[peer], index_buf, True, SENT)

    form(8, 24)

    copy.wait_recv()
    picked = iota((BLOCKS, LANES), 1) == column_of(slot_row)
    names_a = jnp.zeros((BLOCKS, LANES), F32)
    for j in range(N_COL):
        names_a = names_a + jnp.where(column == float(j), index_buf[j, CAP : CAP + 1, :], 0.0)
    key_a = jnp.sum(jnp.where(picked, names_a, 0.0), axis=1, keepdims=True)
    pick_a_true = jnp.where(iota((BLOCKS, IMG_ROW), 1) == key_a, 1.0, 0.0)
    pick_a = pick_a_true.astype(BF16)
    place_a = (
        jnp.concatenate([pick_a_true, jnp.zeros((LANES - BLOCKS, IMG_ROW), F32)], axis=0)
        .T.astype(BF16)
    )
    slots_in = index_buf[...].reshape(SLOTS, LANES)
    slot_lane = iota((SLOTS, LANES), 1)
    slot_sub = lax.broadcasted_iota(jnp.int32, (SLOTS, LANES), 0)
    used = jnp.logical_and(lax.rem(slot_sub, SLOT) < CAP, slots_in == slot_lane)
    cols_row = jnp.concatenate(
        [cols_ref[...].astype(F32), jnp.zeros((1, LANES - BLOCKS), F32)], axis=1
    )
    key_b = jnp.sum(jnp.where(used, cols_row + 1.0, 0.0), axis=1, keepdims=True) - 1.0
    pick_b_true = jnp.where(slot_lane == key_b, 1.0, 0.0)
    pick_b = pick_b_true.astype(BF16)
    place_b = pick_b_true.T.astype(BF16)
    scalar_rows = lax.rem(slot_sub, SLOT) == CAP

    form(24, 32)

    damping = damp_ref[...]
    pad_a = jnp.zeros((LANES - BLOCKS, 256), BF16)

    rhs_b_src[...] = dot(send_hot, terms_b[...].astype(BF16)).reshape(N_COL, SLOT, 256)
    rhs_b_buf[col] = rhs_b_src[col]
    copy_b = exchange(lambda peer: rhs_b_src.at[peer], rhs_b_buf, True, SENT)
    rhs_a_src[...] = dot(
        place_a, jnp.concatenate([terms_a[...].astype(BF16), pad_a], axis=0)
    ).reshape(N_COL, IMG, 256)
    rhs_a_buf[col] = rhs_a_src[col]
    copy_a = exchange(lambda peer: rhs_a_src.at[peer], rhs_a_buf, True)
    form_cross(0, 12)
    copy_b.wait_recv()
    rhs_r_src[...] = dot(place_b, rhs_b_buf[...].reshape(SLOTS, 256).astype(BF16)).reshape(
        N_ROW, IMG, 256
    )
    rhs_r_buf[row] = rhs_r_src[row]
    copy_r = exchange(lambda peer: rhs_r_src.at[peer], rhs_r_buf, False)
    form_cross(12, 22)
    copy_a.wait_recv()
    sums = jnp.sum(rhs_a_buf[...], axis=0)
    copy_r.wait_recv()
    sums = sums + jnp.sum(rhs_r_buf[...], axis=0)
    residual = sums[:, 0:LANES]
    diagonal = damping + sums[:, LANES:256]
    update = jnp.zeros_like(residual)

    row_in_left = lax.broadcasted_iota(jnp.int32, (2 * BLOCKS, LANES), 0)

    def spread(value, slot):
        stacked = jnp.concatenate(halves(value), axis=0)
        for k in range(BLOCKS):
            keep = jnp.logical_or(row_in_left == k, row_in_left == k + BLOCKS)
            left_buf[slot, :, k * LANES : (k + 1) * LANES] = jnp.where(
                keep, stacked, jnp.zeros_like(stacked)
            )

    def products(slot, weight):
        both = dot(left_buf[slot], weight[...])
        return both[0:BLOCKS] + both[BLOCKS : 2 * BLOCKS]

    own = dir_a = dir_b = prod_aa = prod_ca = prod_bb = prod_cb = inner_now = None
    for t in range(ITERS):
        scaled = residual / diagonal
        near_src[t, 0:IMG, :] = scaled
        near_src[t, IMG : IMG + 1, :] = fold(residual * scaled)
        near_buf[t, row] = near_src[t]
        copy_r = exchange(lambda peer: near_src.at[t], near_buf.at[t], False, IMG + 1)
        field_src[t] = scaled
        field_buf[t, col] = scaled
        copy_a = exchange(lambda peer: field_src.at[t], field_buf.at[t], True)

        if t == 0:
            form_cross(22, 32)
        copy_r.wait_recv()
        picks = hot_dot(pick_b, near_buf[t, :, 0:IMG, :].reshape(IMG_COL, LANES))
        norm = jnp.sum(near_buf[t, :, IMG : IMG + 1, :], axis=0)
        pick_src[t] = jnp.where(scalar_rows, norm, picks).reshape(N_COL, SLOT, LANES)
        pick_buf[t, col] = pick_src[t, col]
        copy_b = exchange(lambda peer: pick_src.at[t, peer], pick_buf.at[t], True, SENT)

        copy_a.wait_recv()
        field_a = hot_dot(pick_a, field_buf[t].reshape(IMG_ROW, LANES))
        spread(field_a, 0)
        from_a = products(0, weight_a)

        copy_b.wait_recv()
        received = pick_buf[t].reshape(SLOTS, LANES)
        field_b = hot_dot(take_hot, received)
        spread(field_b, 1)
        from_b = products(1, weight_b)
        inner_next = total_of(jnp.where(scalar_rows, received, 0.0))
        if t == 0:
            own, dir_a, dir_b = scaled, field_a, field_b
            prod_aa, prod_ca, prod_bb = from_a[:, 0:LANES], from_a[:, LANES:256], from_b
        else:
            ratio = inner_next / inner_now
            own = scaled + ratio * own
            dir_a = field_a + ratio * dir_a
            dir_b = field_b + ratio * dir_b
            prod_aa = from_a[:, 0:LANES] + ratio * prod_aa
            prod_ca = from_a[:, LANES:256] + ratio * prod_ca
            prod_bb = from_b + ratio * prod_bb
        inner_now = inner_next
        step_row = fold(dir_a * prod_aa + dir_b * (2.0 * prod_ca + prod_bb)) + fold(
            damping * own * own
        )
        sent = hot_dot(send_hot, prod_ca + prod_bb)
        prod_src[t] = jnp.where(scalar_rows, step_row, sent).reshape(N_COL, SLOT, LANES)
        prod_buf[t, col] = prod_src[t, col]
        copy_b = exchange(lambda peer: prod_src.at[t, peer], prod_buf.at[t], True, SENT)

        from_c = products(1, weight_c)
        prod_cb = from_c if t == 0 else from_c + ratio * prod_cb
        part = hot_dot(
            place_a,
            jnp.concatenate([prod_aa + prod_cb, jnp.zeros((LANES - BLOCKS, LANES), F32)], axis=0),
        )
        part_a_src[t] = part.reshape(N_COL, IMG, LANES)
        part_a_buf[t, col] = part_a_src[t, col]
        copy_a = exchange(lambda peer: part_a_src.at[t, peer], part_a_buf.at[t], True)

        copy_b.wait_recv()
        received = prod_buf[t].reshape(SLOTS, LANES)
        part = hot_dot(place_b, received)
        part_b_src[t, :, 0:IMG, :] = part.reshape(N_ROW, IMG, LANES)
        step_row = fold(jnp.where(scalar_rows, received, 0.0))
        part_b_src[t, :, IMG : IMG + 1, :] = jnp.broadcast_to(step_row, (N_ROW, 1, LANES))
        part_b_buf[t, row] = part_b_src[t, row]
        copy_r = exchange(lambda peer: part_b_src.at[t, peer], part_b_buf.at[t], False, IMG + 1)

        copy_a.wait_recv()
        image = damping * own + jnp.sum(part_a_buf[t], axis=0)
        copy_r.wait_recv()
        sums = jnp.sum(part_b_buf[t, :, 0 : IMG + 1, :], axis=0)
        image = image + sums[0:IMG]
        step_length = inner_now / total_of(sums[IMG : IMG + 1])
        if t < ITERS - 1:
            update = update + step_length * own
            residual = residual - step_length * image
    step = jnp.broadcast_to(step_length, own.shape)
    for i, value in enumerate([update, own, residual, image, step]):
        state_ref[i] = value
    for copy in pending:
        copy.wait_send()


def shards(
    obs_jac,
    rad_jac,
    obs_residual,
    track_damping,
    track_block_column,
    track_slot,
    pair_rows,
    pair_cols,
    image_damping,
):

    def both(*shape, dtype=F32):
        return [pltpu.VMEM(shape, dtype)] * 2

    scratch = [
        pltpu.VMEM(obs_jac.shape, BF16),
        pltpu.VMEM(rad_jac.shape, F32),
        pltpu.VMEM(obs_residual.shape, F32),
        pltpu.VMEM(track_damping.shape, F32),
        pltpu.VMEM((BLOCKS * LANES, 256), BF16),
        *both(BLOCKS * LANES, LANES, dtype=BF16),
        pltpu.VMEM((BLOCKS, LANES, TRACKS), BF16),
        *both(BLOCKS, 256),
        *both(N_COL, SLOT, LANES),
        *both(N_COL, SLOT, 256),
        *both(N_COL, IMG, 256),
        *both(N_ROW, IMG, 256),
        pltpu.VMEM((ITERS, IMG + 8, LANES), F32),
        pltpu.VMEM((ITERS, N_ROW, IMG + 8, LANES), F32),
        pltpu.VMEM((ITERS, IMG, LANES), F32),
        pltpu.VMEM((ITERS, N_COL, IMG, LANES), F32),
        *both(ITERS, N_COL, SLOT, LANES),
        *both(ITERS, N_COL, SLOT, LANES),
        *both(ITERS, N_COL, IMG, LANES),
        *both(ITERS, N_ROW, IMG + 8, LANES),
        pltpu.VMEM((2, 2 * BLOCKS, BLOCKS * LANES), BF16),
        pltpu.SemaphoreType.DMA((3,)),
        pltpu.SemaphoreType.DMA((BLOCKS // STEP,)),
        pltpu.SemaphoreType.DMA((PHASES,)),
        pltpu.SemaphoreType.DMA((PHASES,)),
    ]
    hbm = pl.BlockSpec(memory_space=pltpu.HBM)
    vmem = pl.BlockSpec(memory_space=pltpu.VMEM)
    state = (
        pl.pallas_call(
            kernel,
            out_shape=jax.ShapeDtypeStruct((5, IMG, LANES), F32),
            in_specs=[hbm] * 4 + [vmem] * 5,
            out_specs=vmem,
            scratch_shapes=scratch,
            compiler_params=pltpu.CompilerParams(
                collective_id=0, has_side_effects=True, vmem_limit_bytes=56 * 1024 * 1024
            ),
        )(
            obs_jac,
            rad_jac,
            obs_residual,
            track_damping,
            image_damping,
            track_block_column.reshape(1, BLOCKS),
            track_slot.reshape(1, BLOCKS),
            pair_rows.reshape(1, BLOCKS),
            pair_cols.reshape(1, BLOCKS),
        )
    )
    return state[0] + state[4] * state[1], state[2] - state[4] * state[3]


def solution(mesh):
    in_specs = (
        P(("row", "col"), None, None, None),
        P(("row", "col"), None, None),
        P(("row", "col"), None, None),
        P(("row", "col"), None),
        P(("row", "col"), None),
        P(("row", "col")),
        P(("row", "col")),
        P(("row", "col")),
        P(("row", "col"), None),
    )
    out_specs = (P(("row", "col"), None), P(("row", "col"), None))
    return jax.shard_map(shards, mesh=mesh, in_specs=in_specs, out_specs=out_specs, check_vma=False)
```

```python
import jax
import jax.numpy as jnp
from jax import lax
from jax.experimental import pallas as pl
from jax.experimental.pallas import tpu as pltpu
from jax.sharding import PartitionSpec as P

ITERS = 3
N_ROW = 8
N_COL = 16
BLOCKS = 32
IMG = 16
IMG_ROW = N_COL * IMG
IMG_COL = N_ROW * IMG
LANES = 128
TRACKS = 1024
STEP = 2
CAP = 3
SLOT = 8
SENT = 4
SLOTS = N_COL * SLOT
PHASES = 3 + 1 + 6 * ITERS
MESH = pl.DeviceIdType.MESH
F32 = jnp.float32
BF16 = jnp.bfloat16


def dot(left, right):
    return jnp.dot(left, right, preferred_element_type=F32)


def halves(value):
    high = value.astype(BF16)
    low = (value - high.astype(F32)).astype(BF16)
    return high, low


def hot_dot(hot, value):
    both = dot(hot, jnp.concatenate(halves(value), axis=1))
    return both[:, 0:LANES] + both[:, LANES : 2 * LANES]


def iota(shape, axis):
    return lax.broadcasted_iota(jnp.int32, shape, axis).astype(F32)


def column_of(row_vector):
    n = row_vector.shape[1]
    return jnp.sum(
        jnp.where(iota((n, n), 0) == iota((n, n), 1), row_vector, 0.0), axis=1, keepdims=True
    )


def fold(value):
    return jnp.sum(value, axis=0, keepdims=True)


def total_of(value):
    return jnp.sum(value, axis=(0, 1), keepdims=True)


def spread_row(row):
    tile = jnp.broadcast_to(row, (16, TRACKS)).astype(BF16)
    return jnp.concatenate([tile] * 8, axis=0)


def block_terms(jac0, jac1, rad, resid, damp):
    h0, h1 = rad[0:1, :], rad[1:2, :]
    e0, e1 = resid[0:1, :], resid[1:2, :]
    inverse = 1.0 / (h0 * h0 + h1 * h1 + damp)
    grad = (h0 * e0 + h1 * e1) * inverse
    coef0 = spread_row(1.0 - h0 * h0 * inverse)
    coef1 = spread_row(1.0 - h1 * h1 * inverse)
    coef2 = spread_row(-h0 * h1 * inverse)
    coef3 = jnp.broadcast_to(e0 - h0 * grad, (16, TRACKS)).astype(BF16)
    coef4 = jnp.broadcast_to(e1 - h1 * grad, (16, TRACKS)).astype(BF16)
    jac0_t, jac1_t = jac0.T, jac1.T
    first = dot(jnp.concatenate([coef0 * jac0_t, coef3], axis=0), jac0)
    second = dot(jnp.concatenate([coef1 * jac1_t, coef4], axis=0), jac1)
    first, second = first.astype(BF16), second.astype(BF16)
    block_a, vector_a = first[0:128], first[128:144]
    block_b, vector_b = second[0:128], second[128:144]
    eye = iota((LANES, LANES), 0) == iota((LANES, LANES), 1)
    diag_a = fold(jnp.where(eye, block_a.astype(F32), 0.0))
    diag_b = fold(jnp.where(eye, block_b.astype(F32), 0.0))
    terms_a = jnp.concatenate([vector_a.astype(F32)[0:1], diag_a], axis=1)
    terms_b = jnp.concatenate([vector_b.astype(F32)[0:1], diag_b], axis=1)
    return block_a, block_b, coef2 * jac1_t, terms_a, terms_b


def kernel(
    jac_hbm,
    rad_hbm,
    resid_hbm,
    track_hbm,
    damp_ref,
    column_ref,
    slot_ref,
    rows_ref,
    cols_ref,
    state_ref,
    jac_ref,
    rad_ref,
    resid_ref,
    track_ref,
    weight_a,
    weight_b,
    weight_c,
    cross_ref,
    terms_a,
    terms_b,
    index_src,
    index_buf,
    rhs_b_src,
    rhs_b_buf,
    rhs_a_src,
    rhs_a_buf,
    rhs_r_src,
    rhs_r_buf,
    near_src,
    near_buf,
    field_src,
    field_buf,
    pick_src,
    pick_buf,
    prod_src,
    prod_buf,
    part_a_src,
    part_a_buf,
    part_b_src,
    part_b_buf,
    left_buf,
    load_sem,
    jac_sem,
    send_sem,
    recv_sem,
):
    row, col = lax.axis_index("row"), lax.axis_index("col")

    small = [
        pltpu.make_async_copy(src, dst, load_sem.at[i])
        for i, (src, dst) in enumerate(
            [(rad_hbm, rad_ref), (resid_hbm, resid_ref), (track_hbm, track_ref)]
        )
    ]
    for copy in small:
        copy.start()

    def load(step):
        part = pl.ds(step * STEP, STEP)
        return pltpu.make_async_copy(jac_hbm.at[part], jac_ref.at[part], jac_sem.at[step])

    def start_load(step, carry):
        load(step).start()
        return carry

    lax.fori_loop(0, BLOCKS // STEP, start_load, 0)

    for ref in (index_buf, rhs_b_buf, pick_buf, prod_buf):
        ref[...] = jnp.zeros_like(ref)

    barrier = pltpu.get_barrier_semaphore()

    col_hi, col_lo = lax.div(col, 4), lax.rem(col, 4)
    row_hi, row_lo = lax.div(row, 2), lax.rem(row, 2)
    col_steps = sorted(
        [(i, j) for i in range(4) for j in range(4) if i or j],
        key=lambda step: -sum(min(d, 4 - d) for d in step),
    )
    row_steps = [(i, j) for i in (2, 1, 3, 0) for j in (1, 0) if i or j]
    col_peers = [lax.rem(col_hi + i, 4) * 4 + lax.rem(col_lo + j, 4) for i, j in col_steps]
    row_peers = [lax.rem(row_hi + i, 4) * 2 + lax.rem(row_lo + j, 2) for i, j in row_steps]

    for peer in col_peers:
        pl.semaphore_signal(barrier, inc=1, device_id=(row, peer), device_id_type=MESH)
    for peer in row_peers:
        pl.semaphore_signal(barrier, inc=1, device_id=(peer, col), device_id_type=MESH)

    phases = iter(range(PHASES))
    pending = []

    def exchange(source, target, over_col, rows=None):
        phase = next(phases)
        peers, me = (col_peers, col) if over_col else (row_peers, row)
        rows = pl.ds(0, target.shape[1] if rows is None else rows)
        for peer in peers:
            pltpu.make_async_remote_copy(
                src_ref=source(peer).at[rows],
                dst_ref=target.at[me, rows],
                send_sem=send_sem.at[phase],
                recv_sem=recv_sem.at[phase],
                device_id=(row, peer) if over_col else (peer, col),
                device_id_type=MESH,
            ).start()
        whole = target.at[pl.ds(0, len(peers)), rows]
        copy = pltpu.make_async_remote_copy(
            src_ref=whole,
            dst_ref=whole,
            send_sem=send_sem.at[phase],
            recv_sem=recv_sem.at[phase],
            device_id=(row, peer) if over_col else (peer, col),
            device_id_type=MESH,
        )
        pending.append(copy)
        return copy

    def form(first, last):
        def one(step, carry):
            load(step).wait()
            blocks = [step * STEP + i for i in range(STEP)]
            formed = [
                block_terms(
                    jac_ref[k, 0], jac_ref[k, 1], rad_ref[k], resid_ref[k], track_ref[pl.ds(k, 1), :]
                )
                for k in blocks
            ]
            for k, (block_a, block_b, cross, row_a, row_b) in zip(blocks, formed):
                at = pl.ds(pl.multiple_of(k * LANES, LANES), LANES)
                weight_a[at, 0:LANES] = block_a
                weight_b[at, :] = block_b
                cross_ref[k] = cross
                terms_a[pl.ds(k, 1), :] = row_a
                terms_b[pl.ds(k, 1), :] = row_b
            return carry

        lax.fori_loop(first // STEP, last // STEP, one, 0)

    def form_cross(first, last):
        def one(step, carry):
            blocks = [step * 4 + i for i in range(4)]
            formed = [dot(cross_ref[k], jac_ref[k, 0]).astype(BF16) for k in blocks]
            formed = [(block_c, block_c.T) for block_c in formed]
            for k, (block_c, block_c_t) in zip(blocks, formed):
                at = pl.ds(pl.multiple_of(k * LANES, LANES), LANES)
                weight_c[at, :] = block_c
                weight_a[at, LANES : 2 * LANES] = block_c_t
            return carry

        lax.fori_loop(first // 4, last // 4, one, 0)

    for copy in small:
        copy.wait()
    form(0, 8)

    column_row = column_ref[...].astype(F32)
    slot_row = slot_ref[...].astype(F32)
    column = column_of(column_row)
    same = jnp.logical_and(
        column == column_row, iota((BLOCKS, BLOCKS), 1) < iota((BLOCKS, BLOCKS), 0)
    )
    place = jnp.sum(jnp.where(same, 1.0, 0.0), axis=1, keepdims=True)
    place_col = column * SLOT + place
    place_row = jnp.sum(
        jnp.where(iota((BLOCKS, BLOCKS), 0) == iota((BLOCKS, BLOCKS), 1), place_col, 0.0),
        axis=0,
        keepdims=True,
    )
    send_true = iota((SLOTS, BLOCKS), 0) == place_row
    send_hot = jnp.where(send_true, 1.0, 0.0).astype(BF16)
    take_hot = jnp.where(iota((BLOCKS, SLOTS), 1) == place_col, 1.0, 0.0).astype(BF16)
    slots_out = jnp.sum(jnp.where(send_true, slot_row + 1.0, 0.0), axis=1, keepdims=True) - 1.0
    index_src[...] = jnp.broadcast_to(slots_out, (SLOTS, LANES)).reshape(N_COL, SLOT, LANES)
    for j in range(N_COL):
        index_src[j, CAP : CAP + 1, 0:BLOCKS] = rows_ref[...].astype(F32)
    index_buf[col] = index_src[col]
    pl.semaphore_wait(barrier, N_COL + N_ROW - 2)
    copy = exchange(lambda peer: index_src.at[peer], index_buf, True, SENT)

    form(8, 24)

    copy.wait_recv()
    picked = iota((BLOCKS, LANES), 1) == column_of(slot_row)
    names_a = jnp.zeros((BLOCKS, LANES), F32)
    for j in range(N_COL):
        names_a = names_a + jnp.where(column == float(j), index_buf[j, CAP : CAP + 1, :], 0.0)
    key_a = jnp.sum(jnp.where(picked, names_a, 0.0), axis=1, keepdims=True)
    pick_a_true = jnp.where(iota((BLOCKS, IMG_ROW), 1) == key_a, 1.0, 0.0)
    pick_a = pick_a_true.astype(BF16)
    place_a = (
        jnp.concatenate([pick_a_true, jnp.zeros((LANES - BLOCKS, IMG_ROW), F32)], axis=0)
        .T.astype(BF16)
    )
    slots_in = index_buf[...].reshape(SLOTS, LANES)
    slot_lane = iota((SLOTS, LANES), 1)
    slot_sub = lax.broadcasted_iota(jnp.int32, (SLOTS, LANES), 0)
    used = jnp.logical_and(lax.rem(slot_sub, SLOT) < CAP, slots_in == slot_lane)
    cols_row = jnp.concatenate(
        [cols_ref[...].astype(F32), jnp.zeros((1, LANES - BLOCKS), F32)], axis=1
    )
    key_b = jnp.sum(jnp.where(used, cols_row + 1.0, 0.0), axis=1, keepdims=True) - 1.0
    pick_b_true = jnp.where(slot_lane == key_b, 1.0, 0.0)
    pick_b = pick_b_true.astype(BF16)
    place_b = pick_b_true.T.astype(BF16)
    scalar_rows = lax.rem(slot_sub, SLOT) == CAP

    form(24, 32)

    damping = damp_ref[...]
    pad_a = jnp.zeros((LANES - BLOCKS, 256), BF16)

    rhs_b_src[...] = dot(send_hot, terms_b[...].astype(BF16)).reshape(N_COL, SLOT, 256)
    rhs_b_buf[col] = rhs_b_src[col]
    copy_b = exchange(lambda peer: rhs_b_src.at[peer], rhs_b_buf, True, SENT)
    rhs_a_src[...] = dot(
        place_a, jnp.concatenate([terms_a[...].astype(BF16), pad_a], axis=0)
    ).reshape(N_COL, IMG, 256)
    rhs_a_buf[col] = rhs_a_src[col]
    copy_a = exchange(lambda peer: rhs_a_src.at[peer], rhs_a_buf, True)
    form_cross(0, 12)
    copy_b.wait_recv()
    rhs_r_src[...] = dot(place_b, rhs_b_buf[...].reshape(SLOTS, 256).astype(BF16)).reshape(
        N_ROW, IMG, 256
    )
    rhs_r_buf[row] = rhs_r_src[row]
    copy_r = exchange(lambda peer: rhs_r_src.at[peer], rhs_r_buf, False)
    form_cross(12, 24)
    copy_a.wait_recv()
    sums = jnp.sum(rhs_a_buf[...], axis=0)
    copy_r.wait_recv()
    sums = sums + jnp.sum(rhs_r_buf[...], axis=0)
    residual = sums[:, 0:LANES]
    diagonal = damping + sums[:, LANES:256]
    update = jnp.zeros_like(residual)

    row_in_left = lax.broadcasted_iota(jnp.int32, (2 * BLOCKS, LANES), 0)

    def spread(value, slot):
        stacked = jnp.concatenate(halves(value), axis=0)
        for k in range(BLOCKS):
            keep = jnp.logical_or(row_in_left == k, row_in_left == k + BLOCKS)
            left_buf[slot, :, k * LANES : (k + 1) * LANES] = jnp.where(
                keep, stacked, jnp.zeros_like(stacked)
            )

    def products(slot, weight):
        both = dot(left_buf[slot], weight[...])
        return both[0:BLOCKS] + both[BLOCKS : 2 * BLOCKS]

    own = dir_a = dir_b = prod_aa = prod_ca = prod_bb = prod_cb = inner_now = None
    for t in range(ITERS):
        scaled = residual / diagonal
        near_src[t, 0:IMG, :] = scaled
        near_src[t, IMG : IMG + 1, :] = fold(residual * scaled)
        near_buf[t, row] = near_src[t]
        copy_r = exchange(lambda peer: near_src.at[t], near_buf.at[t], False, IMG + 1)
        field_src[t] = scaled
        field_buf[t, col] = scaled
        copy_a = exchange(lambda peer: field_src.at[t], field_buf.at[t], True)

        if t == 0:
            form_cross(24, 32)
        copy_r.wait_recv()
        picks = hot_dot(pick_b, near_buf[t, :, 0:IMG, :].reshape(IMG_COL, LANES))
        norm = jnp.sum(near_buf[t, :, IMG : IMG + 1, :], axis=0)
        pick_src[t] = jnp.where(scalar_rows, norm, picks).reshape(N_COL, SLOT, LANES)
        pick_buf[t, col] = pick_src[t, col]
        copy_b = exchange(lambda peer: pick_src.at[t, peer], pick_buf.at[t], True, SENT)

        copy_a.wait_recv()
        field_a = hot_dot(pick_a, field_buf[t].reshape(IMG_ROW, LANES))
        spread(field_a, 0)
        from_a = products(0, weight_a)

        copy_b.wait_recv()
        received = pick_buf[t].reshape(SLOTS, LANES)
        field_b = hot_dot(take_hot, received)
        spread(field_b, 1)
        from_b = products(1, weight_b)
        inner_next = total_of(jnp.where(scalar_rows, received, 0.0))
        if t == 0:
            own, dir_a, dir_b = scaled, field_a, field_b
            prod_aa, prod_ca, prod_bb = from_a[:, 0:LANES], from_a[:, LANES:256], from_b
        else:
            ratio = inner_next / inner_now
            own = scaled + ratio * own
            dir_a = field_a + ratio * dir_a
            dir_b = field_b + ratio * dir_b
            prod_aa = from_a[:, 0:LANES] + ratio * prod_aa
            prod_ca = from_a[:, LANES:256] + ratio * prod_ca
            prod_bb = from_b + ratio * prod_bb
        inner_now = inner_next
        step_row = fold(dir_a * prod_aa + dir_b * (2.0 * prod_ca + prod_bb)) + fold(
            damping * own * own
        )
        sent = hot_dot(send_hot, prod_ca + prod_bb)
        prod_src[t] = jnp.where(scalar_rows, step_row, sent).reshape(N_COL, SLOT, LANES)
        prod_buf[t, col] = prod_src[t, col]
        copy_b = exchange(lambda peer: prod_src.at[t, peer], prod_buf.at[t], True, SENT)

        from_c = products(1, weight_c)
        prod_cb = from_c if t == 0 else from_c + ratio * prod_cb
        part = hot_dot(
            place_a,
            jnp.concatenate([prod_aa + prod_cb, jnp.zeros((LANES - BLOCKS, LANES), F32)], axis=0),
        )
        part_a_src[t] = part.reshape(N_COL, IMG, LANES)
        part_a_buf[t, col] = part_a_src[t, col]
        copy_a = exchange(lambda peer: part_a_src.at[t, peer], part_a_buf.at[t], True)

        copy_b.wait_recv()
        received = prod_buf[t].reshape(SLOTS, LANES)
        part = hot_dot(place_b, received)
        part_b_src[t, :, 0:IMG, :] = part.reshape(N_ROW, IMG, LANES)
        step_row = fold(jnp.where(scalar_rows, received, 0.0))
        part_b_src[t, :, IMG : IMG + 1, :] = jnp.broadcast_to(step_row, (N_ROW, 1, LANES))
        part_b_buf[t, row] = part_b_src[t, row]
        copy_r = exchange(lambda peer: part_b_src.at[t, peer], part_b_buf.at[t], False, IMG + 1)

        copy_a.wait_recv()
        image = damping * own + jnp.sum(part_a_buf[t], axis=0)
        copy_r.wait_recv()
        sums = jnp.sum(part_b_buf[t, :, 0 : IMG + 1, :], axis=0)
        image = image + sums[0:IMG]
        step_length = inner_now / total_of(sums[IMG : IMG + 1])
        if t < ITERS - 1:
            update = update + step_length * own
            residual = residual - step_length * image
    step = jnp.broadcast_to(step_length, own.shape)
    for i, value in enumerate([update, own, residual, image, step]):
        state_ref[i] = value
    for copy in pending:
        copy.wait_send()


def shards(
    obs_jac,
    rad_jac,
    obs_residual,
    track_damping,
    track_block_column,
    track_slot,
    pair_rows,
    pair_cols,
    image_damping,
):

    def both(*shape, dtype=F32):
        return [pltpu.VMEM(shape, dtype)] * 2

    scratch = [
        pltpu.VMEM(obs_jac.shape, BF16),
        pltpu.VMEM(rad_jac.shape, F32),
        pltpu.VMEM(obs_residual.shape, F32),
        pltpu.VMEM(track_damping.shape, F32),
        pltpu.VMEM((BLOCKS * LANES, 256), BF16),
        *both(BLOCKS * LANES, LANES, dtype=BF16),
        pltpu.VMEM((BLOCKS, LANES, TRACKS), BF16),
        *both(BLOCKS, 256),
        *both(N_COL, SLOT, LANES),
        *both(N_COL, SLOT, 256),
        *both(N_COL, IMG, 256),
        *both(N_ROW, IMG, 256),
        pltpu.VMEM((ITERS, IMG + 8, LANES), F32),
        pltpu.VMEM((ITERS, N_ROW, IMG + 8, LANES), F32),
        pltpu.VMEM((ITERS, IMG, LANES), F32),
        pltpu.VMEM((ITERS, N_COL, IMG, LANES), F32),
        *both(ITERS, N_COL, SLOT, LANES),
        *both(ITERS, N_COL, SLOT, LANES),
        *both(ITERS, N_COL, IMG, LANES),
        *both(ITERS, N_ROW, IMG + 8, LANES),
        pltpu.VMEM((2, 2 * BLOCKS, BLOCKS * LANES), BF16),
        pltpu.SemaphoreType.DMA((3,)),
        pltpu.SemaphoreType.DMA((BLOCKS // STEP,)),
        pltpu.SemaphoreType.DMA((PHASES,)),
        pltpu.SemaphoreType.DMA((PHASES,)),
    ]
    hbm = pl.BlockSpec(memory_space=pltpu.HBM)
    vmem = pl.BlockSpec(memory_space=pltpu.VMEM)
    state = (
        pl.pallas_call(
            kernel,
            out_shape=jax.ShapeDtypeStruct((5, IMG, LANES), F32),
            in_specs=[hbm] * 4 + [vmem] * 5,
            out_specs=vmem,
            scratch_shapes=scratch,
            compiler_params=pltpu.CompilerParams(
                collective_id=0, has_side_effects=True, vmem_limit_bytes=56 * 1024 * 1024
            ),
        )(
            obs_jac,
            rad_jac,
            obs_residual,
            track_damping,
            image_damping,
            track_block_column.reshape(1, BLOCKS),
            track_slot.reshape(1, BLOCKS),
            pair_rows.reshape(1, BLOCKS),
            pair_cols.reshape(1, BLOCKS),
        )
    )
    return state[0] + state[4] * state[1], state[2] - state[4] * state[3]


def solution(mesh):
    in_specs = (
        P(("row", "col"), None, None, None),
        P(("row", "col"), None, None),
        P(("row", "col"), None, None),
        P(("row", "col"), None),
        P(("row", "col"), None),
        P(("row", "col")),
        P(("row", "col")),
        P(("row", "col")),
        P(("row", "col"), None),
    )
    out_specs = (P(("row", "col"), None), P(("row", "col"), None))
    return jax.shard_map(shards, mesh=mesh, in_specs=in_specs, out_specs=out_specs, check_vma=False)
```

```python
import jax
import jax.numpy as jnp
from jax import lax
from jax.experimental import pallas as pl
from jax.experimental.pallas import tpu as pltpu
from jax.sharding import PartitionSpec as P

ITERS = 3
N_ROW = 8
N_COL = 16
BLOCKS = 32
IMG = 16
IMG_ROW = N_COL * IMG
IMG_COL = N_ROW * IMG
LANES = 128
TRACKS = 1024
STEP = 2
CAP = 3
SLOT = 8
SENT = 4
SLOTS = N_COL * SLOT
PHASES = 3 + 1 + 6 * ITERS
MESH = pl.DeviceIdType.MESH
F32 = jnp.float32
BF16 = jnp.bfloat16


def dot(left, right):
    return jnp.dot(left, right, preferred_element_type=F32)


def halves(value):
    high = value.astype(BF16)
    low = (value - high.astype(F32)).astype(BF16)
    return high, low


def hot_dot(hot, value):
    both = dot(hot, jnp.concatenate(halves(value), axis=1))
    return both[:, 0:LANES] + both[:, LANES : 2 * LANES]


def iota(shape, axis):
    return lax.broadcasted_iota(jnp.int32, shape, axis).astype(F32)


def column_of(row_vector):
    n = row_vector.shape[1]
    return jnp.sum(
        jnp.where(iota((n, n), 0) == iota((n, n), 1), row_vector, 0.0), axis=1, keepdims=True
    )


def fold(value):
    return jnp.sum(value, axis=0, keepdims=True)


def total_of(value):
    return jnp.sum(value, axis=(0, 1), keepdims=True)


def spread_row(row):
    tile = jnp.broadcast_to(row, (16, TRACKS)).astype(BF16)
    return jnp.concatenate([tile] * 8, axis=0)


def block_terms(jac0, jac1, rad, resid, damp):
    h0, h1 = rad[0:1, :], rad[1:2, :]
    e0, e1 = resid[0:1, :], resid[1:2, :]
    inverse = 1.0 / (h0 * h0 + h1 * h1 + damp)
    grad = (h0 * e0 + h1 * e1) * inverse
    coef0 = spread_row(1.0 - h0 * h0 * inverse)
    coef1 = spread_row(1.0 - h1 * h1 * inverse)
    coef2 = spread_row(-h0 * h1 * inverse)
    coef3 = jnp.broadcast_to(e0 - h0 * grad, (16, TRACKS)).astype(BF16)
    coef4 = jnp.broadcast_to(e1 - h1 * grad, (16, TRACKS)).astype(BF16)
    jac0_t, jac1_t = jac0.T, jac1.T
    first = dot(jnp.concatenate([coef0 * jac0_t, coef3], axis=0), jac0)
    second = dot(jnp.concatenate([coef1 * jac1_t, coef4], axis=0), jac1)
    first, second = first.astype(BF16), second.astype(BF16)
    block_a, vector_a = first[0:128], first[128:144]
    block_b, vector_b = second[0:128], second[128:144]
    eye = iota((LANES, LANES), 0) == iota((LANES, LANES), 1)
    diag_a = fold(jnp.where(eye, block_a.astype(F32), 0.0))
    diag_b = fold(jnp.where(eye, block_b.astype(F32), 0.0))
    terms_a = jnp.concatenate([vector_a.astype(F32)[0:1], diag_a], axis=1)
    terms_b = jnp.concatenate([vector_b.astype(F32)[0:1], diag_b], axis=1)
    return block_a, block_b, coef2 * jac1_t, terms_a, terms_b


def kernel(
    jac_hbm,
    rad_hbm,
    resid_hbm,
    track_hbm,
    damp_ref,
    column_ref,
    slot_ref,
    rows_ref,
    cols_ref,
    state_ref,
    jac_ref,
    rad_ref,
    resid_ref,
    track_ref,
    weight_a,
    weight_b,
    weight_c,
    cross_ref,
    terms_a,
    terms_b,
    index_src,
    index_buf,
    rhs_b_src,
    rhs_b_buf,
    rhs_a_src,
    rhs_a_buf,
    rhs_r_src,
    rhs_r_buf,
    near_src,
    near_buf,
    field_src,
    field_buf,
    pick_src,
    pick_buf,
    prod_src,
    prod_buf,
    part_a_src,
    part_a_buf,
    part_b_src,
    part_b_buf,
    left_buf,
    send_hot,
    take_hot,
    pick_a,
    place_a,
    pick_b,
    place_b,
    vector_ref,
    rows_state,
    scalar_ref,
    load_sem,
    jac_sem,
    send_sem,
    recv_sem,
):
    row, col = lax.axis_index("row"), lax.axis_index("col")

    small = [
        pltpu.make_async_copy(src, dst, load_sem.at[i])
        for i, (src, dst) in enumerate(
            [(rad_hbm, rad_ref), (resid_hbm, resid_ref), (track_hbm, track_ref)]
        )
    ]
    for copy in small:
        copy.start()

    def load(step):
        part = pl.ds(step * STEP, STEP)
        return pltpu.make_async_copy(jac_hbm.at[part], jac_ref.at[part], jac_sem.at[step])

    def start_load(step, carry):
        load(step).start()
        return carry

    lax.fori_loop(0, BLOCKS // STEP, start_load, 0)

    for ref in (index_buf, rhs_b_buf, pick_buf, prod_buf):
        ref[...] = jnp.zeros_like(ref)

    barrier = pltpu.get_barrier_semaphore()

    col_hi, col_lo = lax.div(col, 4), lax.rem(col, 4)
    row_hi, row_lo = lax.div(row, 2), lax.rem(row, 2)
    col_steps = sorted(
        [(i, j) for i in range(4) for j in range(4) if i or j],
        key=lambda step: -sum(min(d, 4 - d) for d in step),
    )
    row_steps = [(i, j) for i in (2, 1, 3, 0) for j in (1, 0) if i or j]
    col_peers = [lax.rem(col_hi + i, 4) * 4 + lax.rem(col_lo + j, 4) for i, j in col_steps]
    row_peers = [lax.rem(row_hi + i, 4) * 2 + lax.rem(row_lo + j, 2) for i, j in row_steps]

    for peer in col_peers:
        pl.semaphore_signal(barrier, inc=1, device_id=(row, peer), device_id_type=MESH)
    for peer in row_peers:
        pl.semaphore_signal(barrier, inc=1, device_id=(peer, col), device_id_type=MESH)

    def send(phase, source, target, over_col, rows):
        peers, me = (col_peers, col) if over_col else (row_peers, row)
        for peer in peers:
            pltpu.make_async_remote_copy(
                src_ref=source(peer).at[pl.ds(0, rows)],
                dst_ref=target.at[me, pl.ds(0, rows)],
                send_sem=send_sem.at[phase],
                recv_sem=recv_sem.at[phase],
                device_id=(row, peer) if over_col else (peer, col),
                device_id_type=MESH,
            ).start()

    def waiter(phase, target, over_col, rows):
        peers = col_peers if over_col else row_peers
        whole = target.at[pl.ds(0, len(peers)), pl.ds(0, rows)]
        return pltpu.make_async_remote_copy(
            src_ref=whole,
            dst_ref=whole,
            send_sem=send_sem.at[phase],
            recv_sem=recv_sem.at[phase],
            device_id=(row, peers[0]) if over_col else (peers[0], col),
            device_id_type=MESH,
        )

    def form(step, carry):
        pl.when(step == 4)(send_index)
        pl.when(step == 12)(read_index)
        load(step).wait()
        blocks = [step * STEP + i for i in range(STEP)]
        formed = [
            block_terms(
                jac_ref[k, 0], jac_ref[k, 1], rad_ref[k], resid_ref[k], track_ref[pl.ds(k, 1), :]
            )
            for k in blocks
        ]
        for k, (block_a, block_b, cross, row_a, row_b) in zip(blocks, formed):
            at = pl.ds(pl.multiple_of(k * LANES, LANES), LANES)
            weight_a[at, 0:LANES] = block_a
            weight_b[at, :] = block_b
            cross_ref[k] = cross
            terms_a[pl.ds(k, 1), :] = row_a
            terms_b[pl.ds(k, 1), :] = row_b
        return carry

    def form_cross(first, last):
        def one(step, carry):
            blocks = [step * 4 + i for i in range(4)]
            formed = [dot(cross_ref[k], jac_ref[k, 0]).astype(BF16) for k in blocks]
            formed = [(block_c, block_c.T) for block_c in formed]
            for k, (block_c, block_c_t) in zip(blocks, formed):
                at = pl.ds(pl.multiple_of(k * LANES, LANES), LANES)
                weight_c[at, :] = block_c
                weight_a[at, LANES : 2 * LANES] = block_c_t
            return carry

        lax.fori_loop(first // 4, last // 4, one, 0)

    def block_columns():
        column_row = column_ref[...].astype(F32)
        column = column_of(column_row)
        same = jnp.logical_and(
            column == column_row, iota((BLOCKS, BLOCKS), 1) < iota((BLOCKS, BLOCKS), 0)
        )
        return column, column * SLOT + jnp.sum(jnp.where(same, 1.0, 0.0), axis=1, keepdims=True)

    def send_index():
        column, place_col = block_columns()
        place_row = fold(
            jnp.where(iota((BLOCKS, BLOCKS), 0) == iota((BLOCKS, BLOCKS), 1), place_col, 0.0)
        )
        send_true = iota((SLOTS, BLOCKS), 0) == place_row
        send_hot[...] = jnp.where(send_true, 1.0, 0.0).astype(BF16)
        take_hot[...] = jnp.where(iota((BLOCKS, SLOTS), 1) == place_col, 1.0, 0.0).astype(BF16)
        slot_row = slot_ref[...].astype(F32)
        slots_out = jnp.sum(jnp.where(send_true, slot_row + 1.0, 0.0), axis=1, keepdims=True) - 1.0
        index_src[...] = jnp.broadcast_to(slots_out, (SLOTS, LANES)).reshape(N_COL, SLOT, LANES)
        for j in range(N_COL):
            index_src[j, CAP : CAP + 1, 0:BLOCKS] = rows_ref[...].astype(F32)
        index_buf[col] = index_src[col]
        pl.semaphore_wait(barrier, N_COL + N_ROW - 2)
        send(0, lambda peer: index_src.at[peer], index_buf, True, SENT)

    def read_index():
        waiter(0, index_buf, True, SENT).wait_recv()
        column, _ = block_columns()
        picked = iota((BLOCKS, LANES), 1) == column_of(slot_ref[...].astype(F32))
        names_a = jnp.zeros((BLOCKS, LANES), F32)
        for j in range(N_COL):
            names_a = names_a + jnp.where(column == float(j), index_buf[j, CAP : CAP + 1, :], 0.0)
        key_a = jnp.sum(jnp.where(picked, names_a, 0.0), axis=1, keepdims=True)
        pick = jnp.where(iota((BLOCKS, IMG_ROW), 1) == key_a, 1.0, 0.0)
        pick_a[...] = pick.astype(BF16)
        pick = jnp.concatenate([pick, jnp.zeros((LANES - BLOCKS, IMG_ROW), F32)], axis=0)
        place_a[...] = pick.T.astype(BF16)
        slots_in = index_buf[...].reshape(SLOTS, LANES)
        used = jnp.logical_and(lax.rem(slot_sub, SLOT) < CAP, slots_in == iota((SLOTS, LANES), 1))
        cols_row = jnp.concatenate(
            [cols_ref[...].astype(F32), jnp.zeros((1, LANES - BLOCKS), F32)], axis=1
        )
        key_b = jnp.sum(jnp.where(used, cols_row + 1.0, 0.0), axis=1, keepdims=True) - 1.0
        pick = jnp.where(iota((SLOTS, LANES), 1) == key_b, 1.0, 0.0)
        pick_b[...] = pick.astype(BF16)
        place_b[...] = pick.T.astype(BF16)

    slot_sub = lax.broadcasted_iota(jnp.int32, (SLOTS, LANES), 0)
    scalar_rows = lax.rem(slot_sub, SLOT) == CAP
    for copy in small:
        copy.wait()
    lax.fori_loop(0, BLOCKS // STEP, form, 0)

    damping = damp_ref[...]
    pad_a = jnp.zeros((LANES - BLOCKS, 256), BF16)

    rhs_b_src[...] = dot(send_hot[...], terms_b[...].astype(BF16)).reshape(N_COL, SLOT, 256)
    rhs_b_buf[col] = rhs_b_src[col]
    send(1, lambda peer: rhs_b_src.at[peer], rhs_b_buf, True, SENT)
    rhs_a_src[...] = dot(
        place_a[...], jnp.concatenate([terms_a[...].astype(BF16), pad_a], axis=0)
    ).reshape(N_COL, IMG, 256)
    rhs_a_buf[col] = rhs_a_src[col]
    send(2, lambda peer: rhs_a_src.at[peer], rhs_a_buf, True, IMG)
    form_cross(0, 12)
    waiter(1, rhs_b_buf, True, SENT).wait_recv()
    rhs_r_src[...] = dot(place_b[...], rhs_b_buf[...].reshape(SLOTS, 256).astype(BF16)).reshape(
        N_ROW, IMG, 256
    )
    rhs_r_buf[row] = rhs_r_src[row]
    send(3, lambda peer: rhs_r_src.at[peer], rhs_r_buf, False, IMG)
    form_cross(12, 24)
    waiter(2, rhs_a_buf, True, IMG).wait_recv()
    sums = jnp.sum(rhs_a_buf[...], axis=0)
    waiter(3, rhs_r_buf, False, IMG).wait_recv()
    sums = sums + jnp.sum(rhs_r_buf[...], axis=0)
    right_side = sums[:, 0:LANES]
    diagonal = damping + sums[:, LANES:256]

    row_in_left = lax.broadcasted_iota(jnp.int32, (2 * BLOCKS, LANES), 0)

    def spread(value, slot):
        stacked = jnp.concatenate(halves(value), axis=0)
        for k in range(BLOCKS):
            keep = jnp.logical_or(row_in_left == k, row_in_left == k + BLOCKS)
            left_buf[slot, :, k * LANES : (k + 1) * LANES] = jnp.where(
                keep, stacked, jnp.zeros_like(stacked)
            )

    def products(slot, weight):
        both = dot(left_buf[slot], weight[...])
        return both[0:BLOCKS] + both[BLOCKS : 2 * BLOCKS]

    def exchanges(t):
        return [
            (4 + 6 * t, near_buf.at[t], False, IMG + 1),
            (5 + 6 * t, field_buf.at[t], True, IMG),
            (6 + 6 * t, pick_buf.at[t], True, SENT),
            (7 + 6 * t, prod_buf.at[t], True, SENT),
            (8 + 6 * t, part_a_buf.at[t], True, IMG),
            (9 + 6 * t, part_b_buf.at[t], False, IMG + 1),
        ]

    def iteration(t, carry):
        update, own, residual, image = (vector_ref[i] for i in range(4))
        dir_a, dir_b, *prods = (rows_state[i] for i in range(6))
        step_length, inner_now = scalar_ref[0, 0:1, :], scalar_ref[1, 0:1, :]
        near, field, pick, prod, part_a, part_b = exchanges(t)
        update = update + step_length * own
        residual = residual - step_length * image
        scaled = residual / diagonal
        near_src[t, 0:IMG, :] = scaled
        near_src[t, IMG : IMG + 1, :] = fold(residual * scaled)
        near_buf[t, row] = near_src[t]
        send(near[0], lambda peer: near_src.at[t], *near[1:])
        field_src[t] = scaled
        field_buf[t, col] = scaled
        send(field[0], lambda peer: field_src.at[t], *field[1:])
        pl.when(t == 0)(lambda: form_cross(24, 32))

        waiter(*near).wait_recv()
        picks = hot_dot(pick_b[...], near_buf[t, :, 0:IMG, :].reshape(IMG_COL, LANES))
        norm = jnp.sum(near_buf[t, :, IMG : IMG + 1, :], axis=0)
        pick_src[t] = jnp.where(scalar_rows, norm, picks).reshape(N_COL, SLOT, LANES)
        pick_buf[t, col] = pick_src[t, col]
        send(pick[0], lambda peer: pick_src.at[t, peer], *pick[1:])

        waiter(*field).wait_recv()
        field_a = hot_dot(pick_a[...], field_buf[t].reshape(IMG_ROW, LANES))
        spread(field_a, 0)
        from_a = products(0, weight_a)

        waiter(*pick).wait_recv()
        received = pick_buf[t].reshape(SLOTS, LANES)
        field_b = hot_dot(take_hot[...], received)
        spread(field_b, 1)
        from_b = products(1, weight_b)
        inner_next = total_of(jnp.where(scalar_rows, received, 0.0))
        ratio = jnp.where(t == 0, 0.0, inner_next / inner_now)
        own = scaled + ratio * own
        dir_a = field_a + ratio * dir_a
        dir_b = field_b + ratio * dir_b
        prod_aa, prod_ca, prod_bb, prod_cb = prods
        prod_aa = from_a[:, 0:LANES] + ratio * prod_aa
        prod_ca = from_a[:, LANES:256] + ratio * prod_ca
        prod_bb = from_b + ratio * prod_bb
        step_row = fold(dir_a * prod_aa + dir_b * (2.0 * prod_ca + prod_bb)) + fold(
            damping * own * own
        )
        sent = hot_dot(send_hot[...], prod_ca + prod_bb)
        prod_src[t] = jnp.where(scalar_rows, step_row, sent).reshape(N_COL, SLOT, LANES)
        prod_buf[t, col] = prod_src[t, col]
        send(prod[0], lambda peer: prod_src.at[t, peer], *prod[1:])

        prod_cb = products(1, weight_c) + ratio * prod_cb
        part = hot_dot(
            place_a[...],
            jnp.concatenate([prod_aa + prod_cb, jnp.zeros((LANES - BLOCKS, LANES), F32)], axis=0),
        )
        part_a_src[t] = part.reshape(N_COL, IMG, LANES)
        part_a_buf[t, col] = part_a_src[t, col]
        send(part_a[0], lambda peer: part_a_src.at[t, peer], *part_a[1:])

        waiter(*prod).wait_recv()
        received = prod_buf[t].reshape(SLOTS, LANES)
        part = hot_dot(place_b[...], received)
        part_b_src[t, :, 0:IMG, :] = part.reshape(N_ROW, IMG, LANES)
        step_row = fold(jnp.where(scalar_rows, received, 0.0))
        part_b_src[t, :, IMG : IMG + 1, :] = jnp.broadcast_to(step_row, (N_ROW, 1, LANES))
        part_b_buf[t, row] = part_b_src[t, row]
        send(part_b[0], lambda peer: part_b_src.at[t, peer], *part_b[1:])

        waiter(*part_a).wait_recv()
        image = damping * own + jnp.sum(part_a_buf[t], axis=0)
        waiter(*part_b).wait_recv()
        sums = jnp.sum(part_b_buf[t, :, 0 : IMG + 1, :], axis=0)
        image = image + sums[0:IMG]
        step_length = inner_next / total_of(sums[IMG : IMG + 1])
        for i, value in enumerate([update, own, residual, image]):
            vector_ref[i] = value
        for i, value in enumerate([dir_a, dir_b, prod_aa, prod_ca, prod_bb, prod_cb]):
            rows_state[i] = value
        scalar_ref[0] = jnp.broadcast_to(step_length, (8, LANES))
        scalar_ref[1] = jnp.broadcast_to(inner_next, (8, LANES))
        return carry

    vector_ref[...] = jnp.zeros_like(vector_ref)
    vector_ref[2] = right_side
    rows_state[...] = jnp.zeros_like(rows_state)
    scalar_ref[0] = jnp.zeros((8, LANES), F32)
    scalar_ref[1] = jnp.ones((8, LANES), F32)
    lax.fori_loop(0, ITERS, iteration, 0)
    state_ref[0:4] = vector_ref[...]
    state_ref[4] = jnp.broadcast_to(scalar_ref[0, 0:1, :], (IMG, LANES))

    for sent in (
        (0, index_buf, True, SENT),
        (1, rhs_b_buf, True, SENT),
        (2, rhs_a_buf, True, IMG),
        (3, rhs_r_buf, False, IMG),
    ):
        waiter(*sent).wait_send()

    def drain(t, carry):
        for sent in exchanges(t):
            waiter(*sent).wait_send()
        return carry

    lax.fori_loop(0, ITERS, drain, 0)


def shards(
    obs_jac,
    rad_jac,
    obs_residual,
    track_damping,
    track_block_column,
    track_slot,
    pair_rows,
    pair_cols,
    image_damping,
):

    def both(*shape, dtype=F32):
        return [pltpu.VMEM(shape, dtype)] * 2

    scratch = [
        pltpu.VMEM(obs_jac.shape, BF16),
        pltpu.VMEM(rad_jac.shape, F32),
        pltpu.VMEM(obs_residual.shape, F32),
        pltpu.VMEM(track_damping.shape, F32),
        pltpu.VMEM((BLOCKS * LANES, 256), BF16),
        *both(BLOCKS * LANES, LANES, dtype=BF16),
        pltpu.VMEM((BLOCKS, LANES, TRACKS), BF16),
        *both(BLOCKS, 256),
        *both(N_COL, SLOT, LANES),
        *both(N_COL, SLOT, 256),
        *both(N_COL, IMG, 256),
        *both(N_ROW, IMG, 256),
        pltpu.VMEM((ITERS, IMG + 8, LANES), F32),
        pltpu.VMEM((ITERS, N_ROW, IMG + 8, LANES), F32),
        pltpu.VMEM((ITERS, IMG, LANES), F32),
        pltpu.VMEM((ITERS, N_COL, IMG, LANES), F32),
        *both(ITERS, N_COL, SLOT, LANES),
        *both(ITERS, N_COL, SLOT, LANES),
        *both(ITERS, N_COL, IMG, LANES),
        *both(ITERS, N_ROW, IMG + 8, LANES),
        pltpu.VMEM((2, 2 * BLOCKS, BLOCKS * LANES), BF16),
        pltpu.VMEM((SLOTS, BLOCKS), BF16),
        pltpu.VMEM((BLOCKS, SLOTS), BF16),
        pltpu.VMEM((BLOCKS, IMG_ROW), BF16),
        pltpu.VMEM((IMG_ROW, LANES), BF16),
        *both(SLOTS, LANES, dtype=BF16),
        pltpu.VMEM((4, IMG, LANES), F32),
        pltpu.VMEM((6, BLOCKS, LANES), F32),
        pltpu.VMEM((2, 8, LANES), F32),
        pltpu.SemaphoreType.DMA((3,)),
        pltpu.SemaphoreType.DMA((BLOCKS // STEP,)),
        pltpu.SemaphoreType.DMA((PHASES,)),
        pltpu.SemaphoreType.DMA((PHASES,)),
    ]
    hbm = pl.BlockSpec(memory_space=pltpu.HBM)
    vmem = pl.BlockSpec(memory_space=pltpu.VMEM)
    state = (
        pl.pallas_call(
            kernel,
            out_shape=jax.ShapeDtypeStruct((5, IMG, LANES), F32),
            in_specs=[hbm] * 4 + [vmem] * 5,
            out_specs=vmem,
            scratch_shapes=scratch,
            compiler_params=pltpu.CompilerParams(
                collective_id=0, has_side_effects=True, vmem_limit_bytes=56 * 1024 * 1024
            ),
        )(
            obs_jac,
            rad_jac,
            obs_residual,
            track_damping,
            image_damping,
            track_block_column.reshape(1, BLOCKS),
            track_slot.reshape(1, BLOCKS),
            pair_rows.reshape(1, BLOCKS),
            pair_cols.reshape(1, BLOCKS),
        )
    )
    return state[0] + state[4] * state[1], state[2] - state[4] * state[3]


def solution(mesh):
    in_specs = (
        P(("row", "col"), None, None, None),
        P(("row", "col"), None, None),
        P(("row", "col"), None, None),
        P(("row", "col"), None),
        P(("row", "col"), None),
        P(("row", "col")),
        P(("row", "col")),
        P(("row", "col")),
        P(("row", "col"), None),
    )
    out_specs = (P(("row", "col"), None), P(("row", "col"), None))
    return jax.shard_map(shards, mesh=mesh, in_specs=in_specs, out_specs=out_specs, check_vma=False)
```

```python
import jax
import jax.numpy as jnp
from jax import lax
from jax.experimental import pallas as pl
from jax.experimental.pallas import tpu as pltpu
from jax.sharding import PartitionSpec as P

ITERS = 3
N_ROW = 8
N_COL = 16
BLOCKS = 32
IMG = 16
IMG_ROW = N_COL * IMG
IMG_COL = N_ROW * IMG
LANES = 128
TRACKS = 1024
STEP = 2
CAP = 3
SLOT = 8
SENT = 4
SLOTS = N_COL * SLOT
PHASES = 5 + 8 * ITERS
MESH = pl.DeviceIdType.MESH
F32 = jnp.float32
BF16 = jnp.bfloat16


def dot(left, right):
    return jnp.dot(left, right, preferred_element_type=F32)


def halves(value):
    high = value.astype(BF16)
    low = (value - high.astype(F32)).astype(BF16)
    return high, low


def hot_dot(hot, value):
    both = dot(hot, jnp.concatenate(halves(value), axis=1))
    return both[:, 0:LANES] + both[:, LANES : 2 * LANES]


def iota(shape, axis):
    return lax.broadcasted_iota(jnp.int32, shape, axis).astype(F32)


def column_of(row_vector):
    n = row_vector.shape[1]
    return jnp.sum(
        jnp.where(iota((n, n), 0) == iota((n, n), 1), row_vector, 0.0), axis=1, keepdims=True
    )


def fold(value):
    return jnp.sum(value, axis=0, keepdims=True)


def total_of(value):
    return jnp.sum(value, axis=(0, 1), keepdims=True)


def spread_row(row):
    tile = jnp.broadcast_to(row, (16, TRACKS)).astype(BF16)
    return jnp.concatenate([tile] * 8, axis=0)


def block_terms(jac0, jac1, rad, resid, damp):
    h0, h1 = rad[0:1, :], rad[1:2, :]
    e0, e1 = resid[0:1, :], resid[1:2, :]
    inverse = 1.0 / (h0 * h0 + h1 * h1 + damp)
    grad = (h0 * e0 + h1 * e1) * inverse
    coef0 = spread_row(1.0 - h0 * h0 * inverse)
    coef1 = spread_row(1.0 - h1 * h1 * inverse)
    coef2 = spread_row(-h0 * h1 * inverse)
    coef3 = jnp.broadcast_to(e0 - h0 * grad, (16, TRACKS)).astype(BF16)
    coef4 = jnp.broadcast_to(e1 - h1 * grad, (16, TRACKS)).astype(BF16)
    jac0_t, jac1_t = jac0.T, jac1.T
    first = dot(jnp.concatenate([coef0 * jac0_t, coef3], axis=0), jac0)
    second = dot(jnp.concatenate([coef1 * jac1_t, coef4], axis=0), jac1)
    first, second = first.astype(BF16), second.astype(BF16)
    block_a, vector_a = first[0:128], first[128:144]
    block_b, vector_b = second[0:128], second[128:144]
    eye = iota((LANES, LANES), 0) == iota((LANES, LANES), 1)
    diag_a = fold(jnp.where(eye, block_a.astype(F32), 0.0))
    diag_b = fold(jnp.where(eye, block_b.astype(F32), 0.0))
    terms_a = jnp.concatenate([vector_a.astype(F32)[0:1], diag_a], axis=1)
    terms_b = jnp.concatenate([vector_b.astype(F32)[0:1], diag_b], axis=1)
    return block_a, block_b, coef2 * jac1_t, terms_a, terms_b


def kernel(
    jac_hbm,
    rad_hbm,
    resid_hbm,
    track_hbm,
    damp_ref,
    column_ref,
    slot_ref,
    rows_ref,
    cols_ref,
    state_ref,
    jac_ref,
    rad_ref,
    resid_ref,
    track_ref,
    weight_a,
    weight_b,
    weight_c,
    cross_ref,
    terms_a,
    terms_b,
    index_src,
    index_buf,
    rhs_b_src,
    rhs_b_buf,
    rhs_a_src,
    rhs_a_buf,
    rhs_m_src,
    rhs_m_buf,
    rhs_r_src,
    rhs_r_buf,
    near_src,
    near_buf,
    field_src,
    field_buf,
    pick_src,
    pick_buf,
    prod_src,
    prod_buf,
    part_a_src,
    part_a_buf,
    part_m_src,
    part_m_buf,
    part_b_src,
    part_b_buf,
    left_buf,
    send_hot,
    take_hot,
    pick_a,
    place_a,
    pick_b,
    place_b,
    vector_ref,
    rows_state,
    scalar_ref,
    load_sem,
    jac_sem,
    send_sem,
    recv_sem,
):
    row, col = lax.axis_index("row"), lax.axis_index("col")

    small = [
        pltpu.make_async_copy(src, dst, load_sem.at[i])
        for i, (src, dst) in enumerate(
            [(rad_hbm, rad_ref), (resid_hbm, resid_ref), (track_hbm, track_ref)]
        )
    ]
    for copy in small:
        copy.start()

    def load(step):
        part = pl.ds(step * STEP, STEP)
        return pltpu.make_async_copy(jac_hbm.at[part], jac_ref.at[part], jac_sem.at[step])

    def start_load(step, carry):
        load(step).start()
        return carry

    lax.fori_loop(0, BLOCKS // STEP, start_load, 0)

    for ref in (index_buf, rhs_b_buf, pick_buf, prod_buf):
        ref[...] = jnp.zeros_like(ref)

    barrier = pltpu.get_barrier_semaphore()

    col_hi, col_lo = lax.div(col, 4), lax.rem(col, 4)
    row_hi, row_lo = lax.div(row, 2), lax.rem(row, 2)
    col_steps = sorted(
        [(i, j) for i in range(4) for j in range(4) if i or j],
        key=lambda step: -sum(min(d, 4 - d) for d in step),
    )
    row_steps = [(i, j) for i in (2, 1, 3, 0) for j in (1, 0) if i or j]
    col_peers = [lax.rem(col_hi + i, 4) * 4 + lax.rem(col_lo + j, 4) for i, j in col_steps]
    row_peers = [lax.rem(row_hi + i, 4) * 2 + lax.rem(row_lo + j, 2) for i, j in row_steps]

    for peer in col_peers:
        pl.semaphore_signal(barrier, inc=1, device_id=(row, peer), device_id_type=MESH)
    for peer in row_peers:
        pl.semaphore_signal(barrier, inc=1, device_id=(peer, col), device_id_type=MESH)

    def send(phase, source, target, over_col, rows):
        peers, me = (col_peers, col) if over_col else (row_peers, row)
        for peer in peers:
            pltpu.make_async_remote_copy(
                src_ref=source(peer).at[pl.ds(0, rows)],
                dst_ref=target.at[me, pl.ds(0, rows)],
                send_sem=send_sem.at[phase],
                recv_sem=recv_sem.at[phase],
                device_id=(row, peer) if over_col else (peer, col),
                device_id_type=MESH,
            ).start()

    def waiter(phase, target, over_col, rows):
        peers = col_peers if over_col else row_peers
        whole = target.at[pl.ds(0, len(peers)), pl.ds(0, rows)]
        return pltpu.make_async_remote_copy(
            src_ref=whole,
            dst_ref=whole,
            send_sem=send_sem.at[phase],
            recv_sem=recv_sem.at[phase],
            device_id=(row, peers[0]) if over_col else (peers[0], col),
            device_id_type=MESH,
        )

    def form(step, carry):
        pl.when(step == 4)(send_index)
        pl.when(step == 12)(read_index)
        load(step).wait()
        blocks = [step * STEP + i for i in range(STEP)]
        formed = [
            block_terms(
                jac_ref[k, 0], jac_ref[k, 1], rad_ref[k], resid_ref[k], track_ref[pl.ds(k, 1), :]
            )
            for k in blocks
        ]
        for k, (block_a, block_b, cross, row_a, row_b) in zip(blocks, formed):
            at = pl.ds(pl.multiple_of(k * LANES, LANES), LANES)
            weight_a[at, 0:LANES] = block_a
            weight_b[at, :] = block_b
            cross_ref[k] = cross
            terms_a[pl.ds(k, 1), :] = row_a
            terms_b[pl.ds(k, 1), :] = row_b
        return carry

    def form_cross(first, last):
        def one(step, carry):
            blocks = [step * 4 + i for i in range(4)]
            formed = [dot(cross_ref[k], jac_ref[k, 0]).astype(BF16) for k in blocks]
            formed = [(block_c, block_c.T) for block_c in formed]
            for k, (block_c, block_c_t) in zip(blocks, formed):
                at = pl.ds(pl.multiple_of(k * LANES, LANES), LANES)
                weight_c[at, :] = block_c
                weight_a[at, LANES : 2 * LANES] = block_c_t
            return carry

        lax.fori_loop(first // 4, last // 4, one, 0)

    lo_group = [(lax.rem(col_lo + j, 4), (row, col_hi * 4 + lax.rem(col_lo + j, 4))) for j in (2, 1, 3)]
    hi_group = [(lax.rem(col_hi + i, 4), (row, lax.rem(col_hi + i, 4) * 4 + col_lo)) for i in (2, 1, 3)]
    slab = pl.ds(col_hi * 4, 4)

    def relay(phase, group, source, target):
        for index, device in group:
            pltpu.make_async_remote_copy(
                src_ref=source(index),
                dst_ref=target,
                send_sem=send_sem.at[phase],
                recv_sem=recv_sem.at[phase],
                device_id=device,
                device_id_type=MESH,
            ).start()

    def relayed(phase, whole):
        return pltpu.make_async_remote_copy(
            src_ref=whole,
            dst_ref=whole,
            send_sem=send_sem.at[phase],
            recv_sem=recv_sem.at[phase],
            device_id=lo_group[0][1],
            device_id_type=MESH,
        )

    def block_columns():
        column_row = column_ref[...].astype(F32)
        column = column_of(column_row)
        same = jnp.logical_and(
            column == column_row, iota((BLOCKS, BLOCKS), 1) < iota((BLOCKS, BLOCKS), 0)
        )
        return column, column * SLOT + jnp.sum(jnp.where(same, 1.0, 0.0), axis=1, keepdims=True)

    def send_index():
        column, place_col = block_columns()
        place_row = fold(
            jnp.where(iota((BLOCKS, BLOCKS), 0) == iota((BLOCKS, BLOCKS), 1), place_col, 0.0)
        )
        send_true = iota((SLOTS, BLOCKS), 0) == place_row
        send_hot[...] = jnp.where(send_true, 1.0, 0.0).astype(BF16)
        take_hot[...] = jnp.where(iota((BLOCKS, SLOTS), 1) == place_col, 1.0, 0.0).astype(BF16)
        slot_row = slot_ref[...].astype(F32)
        slots_out = jnp.sum(jnp.where(send_true, slot_row + 1.0, 0.0), axis=1, keepdims=True) - 1.0
        index_src[...] = jnp.broadcast_to(slots_out, (SLOTS, LANES)).reshape(N_COL, SLOT, LANES)
        for j in range(N_COL):
            index_src[j, CAP : CAP + 1, 0:BLOCKS] = rows_ref[...].astype(F32)
        index_buf[col] = index_src[col]
        pl.semaphore_wait(barrier, N_COL + N_ROW - 2)
        send(0, lambda peer: index_src.at[peer], index_buf, True, SENT)

    def read_index():
        waiter(0, index_buf, True, SENT).wait_recv()
        column, _ = block_columns()
        picked = iota((BLOCKS, LANES), 1) == column_of(slot_ref[...].astype(F32))
        names_a = jnp.zeros((BLOCKS, LANES), F32)
        for j in range(N_COL):
            names_a = names_a + jnp.where(column == float(j), index_buf[j, CAP : CAP + 1, :], 0.0)
        key_a = jnp.sum(jnp.where(picked, names_a, 0.0), axis=1, keepdims=True)
        pick = jnp.where(iota((BLOCKS, IMG_ROW), 1) == key_a, 1.0, 0.0)
        pick_a[...] = pick.astype(BF16)
        pick = jnp.concatenate([pick, jnp.zeros((LANES - BLOCKS, IMG_ROW), F32)], axis=0)
        place_a[...] = pick.T.astype(BF16)
        slots_in = index_buf[...].reshape(SLOTS, LANES)
        used = jnp.logical_and(lax.rem(slot_sub, SLOT) < CAP, slots_in == iota((SLOTS, LANES), 1))
        cols_row = jnp.concatenate(
            [cols_ref[...].astype(F32), jnp.zeros((1, LANES - BLOCKS), F32)], axis=1
        )
        key_b = jnp.sum(jnp.where(used, cols_row + 1.0, 0.0), axis=1, keepdims=True) - 1.0
        pick = jnp.where(iota((SLOTS, LANES), 1) == key_b, 1.0, 0.0)
        pick_b[...] = pick.astype(BF16)
        place_b[...] = pick.T.astype(BF16)

    slot_sub = lax.broadcasted_iota(jnp.int32, (SLOTS, LANES), 0)
    scalar_rows = lax.rem(slot_sub, SLOT) == CAP
    for copy in small:
        copy.wait()
    lax.fori_loop(0, BLOCKS // STEP, form, 0)

    damping = damp_ref[...]
    pad_a = jnp.zeros((LANES - BLOCKS, 256), BF16)

    rhs_b_src[...] = dot(send_hot[...], terms_b[...].astype(BF16)).reshape(N_COL, SLOT, 256)
    rhs_b_buf[col] = rhs_b_src[col]
    send(1, lambda peer: rhs_b_src.at[peer], rhs_b_buf, True, SENT)
    rhs_a_src[...] = dot(
        place_a[...], jnp.concatenate([terms_a[...].astype(BF16), pad_a], axis=0)
    ).reshape(N_COL, IMG, 256)
    rhs_a_buf[col_hi] = rhs_a_src[slab]
    relay(2, hi_group, lambda i: rhs_a_src.at[pl.ds(i * 4, 4)], rhs_a_buf.at[col_hi])
    form_cross(0, 12)
    waiter(1, rhs_b_buf, True, SENT).wait_recv()
    rhs_r_src[...] = dot(place_b[...], rhs_b_buf[...].reshape(SLOTS, 256).astype(BF16)).reshape(
        N_ROW, IMG, 256
    )
    rhs_r_buf[row] = rhs_r_src[row]
    send(3, lambda peer: rhs_r_src.at[peer], rhs_r_buf, False, IMG)
    relayed(2, rhs_a_buf.at[pl.ds(0, 3)]).wait_recv()
    rhs_m_src[...] = jnp.sum(rhs_a_buf[...], axis=0)
    rhs_m_buf[col_lo] = rhs_m_src[col_lo]
    relay(4, lo_group, lambda j: rhs_m_src.at[j], rhs_m_buf.at[col_lo])
    form_cross(12, 24)
    relayed(4, rhs_m_buf.at[pl.ds(0, 3)]).wait_recv()
    sums = jnp.sum(rhs_m_buf[...], axis=0)
    waiter(3, rhs_r_buf, False, IMG).wait_recv()
    sums = sums + jnp.sum(rhs_r_buf[...], axis=0)
    right_side = sums[:, 0:LANES]
    diagonal = damping + sums[:, LANES:256]

    row_in_left = lax.broadcasted_iota(jnp.int32, (2 * BLOCKS, LANES), 0)

    def spread(value, slot):
        stacked = jnp.concatenate(halves(value), axis=0)
        for k in range(BLOCKS):
            keep = jnp.logical_or(row_in_left == k, row_in_left == k + BLOCKS)
            left_buf[slot, :, k * LANES : (k + 1) * LANES] = jnp.where(
                keep, stacked, jnp.zeros_like(stacked)
            )

    def products(slot, weight):
        both = dot(left_buf[slot], weight[...])
        return both[0:BLOCKS] + both[BLOCKS : 2 * BLOCKS]

    def exchanges(t):
        first = 5 + 8 * t
        return [
            (first, near_buf.at[t], False, IMG + 1),
            (first + 1, pick_buf.at[t], True, SENT),
            (first + 2, prod_buf.at[t], True, SENT),
            (first + 3, part_b_buf.at[t], False, IMG + 1),
        ], [
            (first + 4, field_buf.at[t, pl.ds(0, 3)]),
            (first + 5, field_buf.at[t, pl.ds(0, 12)]),
            (first + 6, part_a_buf.at[t, pl.ds(0, 3)]),
            (first + 7, part_m_buf.at[t, pl.ds(0, 3)]),
        ]

    def iteration(t, carry):
        update, own, residual, image = (vector_ref[i] for i in range(4))
        dir_a, dir_b, *prods = (rows_state[i] for i in range(6))
        step_length, inner_now = scalar_ref[0, 0:1, :], scalar_ref[1, 0:1, :]
        (near, pick, prod, part_b), (field_x, field_z, part_z, part_x) = exchanges(t)
        update = update + step_length * own
        residual = residual - step_length * image
        scaled = residual / diagonal
        near_src[t, 0:IMG, :] = scaled
        near_src[t, IMG : IMG + 1, :] = fold(residual * scaled)
        near_buf[t, row] = near_src[t]
        send(near[0], lambda peer: near_src.at[t], *near[1:])
        field_src[t] = scaled
        field_buf[t, col] = scaled
        relay(field_x[0], lo_group, lambda j: field_src.at[t], field_buf.at[t, col])
        pl.when(t == 0)(lambda: form_cross(24, 32))
        relayed(*field_x).wait_recv()
        relay(field_z[0], hi_group, lambda i: field_buf.at[t, slab], field_buf.at[t, slab])

        waiter(*near).wait_recv()
        picks = hot_dot(pick_b[...], near_buf[t, :, 0:IMG, :].reshape(IMG_COL, LANES))
        norm = jnp.sum(near_buf[t, :, IMG : IMG + 1, :], axis=0)
        pick_src[t] = jnp.where(scalar_rows, norm, picks).reshape(N_COL, SLOT, LANES)
        pick_buf[t, col] = pick_src[t, col]
        send(pick[0], lambda peer: pick_src.at[t, peer], *pick[1:])

        relayed(*field_z).wait_recv()
        field_a = hot_dot(pick_a[...], field_buf[t].reshape(IMG_ROW, LANES))
        spread(field_a, 0)
        from_a = products(0, weight_a)

        waiter(*pick).wait_recv()
        received = pick_buf[t].reshape(SLOTS, LANES)
        field_b = hot_dot(take_hot[...], received)
        spread(field_b, 1)
        from_b = products(1, weight_b)
        inner_next = total_of(jnp.where(scalar_rows, received, 0.0))
        ratio = jnp.where(t == 0, 0.0, inner_next / inner_now)
        own = scaled + ratio * own
        dir_a = field_a + ratio * dir_a
        dir_b = field_b + ratio * dir_b
        prod_aa, prod_ca, prod_bb, prod_cb = prods
        prod_aa = from_a[:, 0:LANES] + ratio * prod_aa
        prod_ca = from_a[:, LANES:256] + ratio * prod_ca
        prod_bb = from_b + ratio * prod_bb
        step_row = fold(dir_a * prod_aa + dir_b * (2.0 * prod_ca + prod_bb)) + fold(
            damping * own * own
        )
        sent = hot_dot(send_hot[...], prod_ca + prod_bb)
        prod_src[t] = jnp.where(scalar_rows, step_row, sent).reshape(N_COL, SLOT, LANES)
        prod_buf[t, col] = prod_src[t, col]
        send(prod[0], lambda peer: prod_src.at[t, peer], *prod[1:])

        prod_cb = products(1, weight_c) + ratio * prod_cb
        part = hot_dot(
            place_a[...],
            jnp.concatenate([prod_aa + prod_cb, jnp.zeros((LANES - BLOCKS, LANES), F32)], axis=0),
        )
        part_a_src[t] = part.reshape(N_COL, IMG, LANES)
        part_a_buf[t, col_hi] = part_a_src[t, slab]
        relay(
            part_z[0], hi_group, lambda i: part_a_src.at[t, pl.ds(i * 4, 4)], part_a_buf.at[t, col_hi]
        )

        waiter(*prod).wait_recv()
        received = prod_buf[t].reshape(SLOTS, LANES)
        part = hot_dot(place_b[...], received)
        part_b_src[t, :, 0:IMG, :] = part.reshape(N_ROW, IMG, LANES)
        step_row = fold(jnp.where(scalar_rows, received, 0.0))
        part_b_src[t, :, IMG : IMG + 1, :] = jnp.broadcast_to(step_row, (N_ROW, 1, LANES))
        part_b_buf[t, row] = part_b_src[t, row]
        send(part_b[0], lambda peer: part_b_src.at[t, peer], *part_b[1:])

        relayed(*part_z).wait_recv()
        part_m_src[t] = jnp.sum(part_a_buf[t], axis=0)
        part_m_buf[t, col_lo] = part_m_src[t, col_lo]
        relay(part_x[0], lo_group, lambda j: part_m_src.at[t, j], part_m_buf.at[t, col_lo])
        relayed(*part_x).wait_recv()
        image = damping * own + jnp.sum(part_m_buf[t], axis=0)
        waiter(*part_b).wait_recv()
        sums = jnp.sum(part_b_buf[t, :, 0 : IMG + 1, :], axis=0)
        image = image + sums[0:IMG]
        step_length = inner_next / total_of(sums[IMG : IMG + 1])
        for i, value in enumerate([update, own, residual, image]):
            vector_ref[i] = value
        for i, value in enumerate([dir_a, dir_b, prod_aa, prod_ca, prod_bb, prod_cb]):
            rows_state[i] = value
        scalar_ref[0] = jnp.broadcast_to(step_length, (8, LANES))
        scalar_ref[1] = jnp.broadcast_to(inner_next, (8, LANES))
        return carry

    vector_ref[...] = jnp.zeros_like(vector_ref)
    vector_ref[2] = right_side
    rows_state[...] = jnp.zeros_like(rows_state)
    scalar_ref[0] = jnp.zeros((8, LANES), F32)
    scalar_ref[1] = jnp.ones((8, LANES), F32)
    lax.fori_loop(0, ITERS, iteration, 0)
    state_ref[0:4] = vector_ref[...]
    state_ref[4] = jnp.broadcast_to(scalar_ref[0, 0:1, :], (IMG, LANES))

    for sent in (
        (0, index_buf, True, SENT),
        (1, rhs_b_buf, True, SENT),
        (3, rhs_r_buf, False, IMG),
    ):
        waiter(*sent).wait_send()
    relayed(2, rhs_a_buf.at[pl.ds(0, 3)]).wait_send()
    relayed(4, rhs_m_buf.at[pl.ds(0, 3)]).wait_send()

    def drain(t, carry):
        whole, stages = exchanges(t)
        for sent in whole:
            waiter(*sent).wait_send()
        for sent in stages:
            relayed(*sent).wait_send()
        return carry

    lax.fori_loop(0, ITERS, drain, 0)


def shards(
    obs_jac,
    rad_jac,
    obs_residual,
    track_damping,
    track_block_column,
    track_slot,
    pair_rows,
    pair_cols,
    image_damping,
):

    def both(*shape, dtype=F32):
        return [pltpu.VMEM(shape, dtype)] * 2

    scratch = [
        pltpu.VMEM(obs_jac.shape, BF16),
        pltpu.VMEM(rad_jac.shape, F32),
        pltpu.VMEM(obs_residual.shape, F32),
        pltpu.VMEM(track_damping.shape, F32),
        pltpu.VMEM((BLOCKS * LANES, 256), BF16),
        *both(BLOCKS * LANES, LANES, dtype=BF16),
        pltpu.VMEM((BLOCKS, LANES, TRACKS), BF16),
        *both(BLOCKS, 256),
        *both(N_COL, SLOT, LANES),
        *both(N_COL, SLOT, 256),
        pltpu.VMEM((N_COL, IMG, 256), F32),
        pltpu.VMEM((4, 4, IMG, 256), F32),
        *both(4, IMG, 256),
        *both(N_ROW, IMG, 256),
        pltpu.VMEM((ITERS, IMG + 8, LANES), F32),
        pltpu.VMEM((ITERS, N_ROW, IMG + 8, LANES), F32),
        pltpu.VMEM((ITERS, IMG, LANES), F32),
        pltpu.VMEM((ITERS, N_COL, IMG, LANES), F32),
        *both(ITERS, N_COL, SLOT, LANES),
        *both(ITERS, N_COL, SLOT, LANES),
        pltpu.VMEM((ITERS, N_COL, IMG, LANES), F32),
        pltpu.VMEM((ITERS, 4, 4, IMG, LANES), F32),
        *both(ITERS, 4, IMG, LANES),
        *both(ITERS, N_ROW, IMG + 8, LANES),
        pltpu.VMEM((2, 2 * BLOCKS, BLOCKS * LANES), BF16),
        pltpu.VMEM((SLOTS, BLOCKS), BF16),
        pltpu.VMEM((BLOCKS, SLOTS), BF16),
        pltpu.VMEM((BLOCKS, IMG_ROW), BF16),
        pltpu.VMEM((IMG_ROW, LANES), BF16),
        *both(SLOTS, LANES, dtype=BF16),
        pltpu.VMEM((4, IMG, LANES), F32),
        pltpu.VMEM((6, BLOCKS, LANES), F32),
        pltpu.VMEM((2, 8, LANES), F32),
        pltpu.SemaphoreType.DMA((3,)),
        pltpu.SemaphoreType.DMA((BLOCKS // STEP,)),
        pltpu.SemaphoreType.DMA((PHASES,)),
        pltpu.SemaphoreType.DMA((PHASES,)),
    ]
    hbm = pl.BlockSpec(memory_space=pltpu.HBM)
    vmem = pl.BlockSpec(memory_space=pltpu.VMEM)
    state = (
        pl.pallas_call(
            kernel,
            out_shape=jax.ShapeDtypeStruct((5, IMG, LANES), F32),
            in_specs=[hbm] * 4 + [vmem] * 5,
            out_specs=vmem,
            scratch_shapes=scratch,
            compiler_params=pltpu.CompilerParams(
                collective_id=0, has_side_effects=True, vmem_limit_bytes=56 * 1024 * 1024
            ),
        )(
            obs_jac,
            rad_jac,
            obs_residual,
            track_damping,
            image_damping,
            track_block_column.reshape(1, BLOCKS),
            track_slot.reshape(1, BLOCKS),
            pair_rows.reshape(1, BLOCKS),
            pair_cols.reshape(1, BLOCKS),
        )
    )
    return state[0] + state[4] * state[1], state[2] - state[4] * state[3]


def solution(mesh):
    in_specs = (
        P(("row", "col"), None, None, None),
        P(("row", "col"), None, None),
        P(("row", "col"), None, None),
        P(("row", "col"), None),
        P(("row", "col"), None),
        P(("row", "col")),
        P(("row", "col")),
        P(("row", "col")),
        P(("row", "col"), None),
    )
    out_specs = (P(("row", "col"), None), P(("row", "col"), None))
    return jax.shard_map(shards, mesh=mesh, in_specs=in_specs, out_specs=out_specs, check_vma=False)
```

```python
import jax
import jax.numpy as jnp
from jax import lax
from jax.experimental import pallas as pl
from jax.experimental.pallas import tpu as pltpu
from jax.sharding import PartitionSpec as P

ITERS = 3
N_ROW = 8
N_COL = 16
BLOCKS = 32
IMG = 16
IMG_ROW = N_COL * IMG
IMG_COL = N_ROW * IMG
LANES = 128
TRACKS = 1024
STEP = 2
CAP = 3
AHEAD = 4
SLOT = 8
SENT = 4
SLOTS = N_COL * SLOT
PHASES = 3 + 1 + 6 * ITERS
MESH = pl.DeviceIdType.MESH
F32 = jnp.float32
BF16 = jnp.bfloat16


def dot(left, right):
    return jnp.dot(left, right, preferred_element_type=F32)


def halves(value):
    high = value.astype(BF16)
    low = (value - high.astype(F32)).astype(BF16)
    return high, low


def hot_dot(hot, value):
    both = dot(hot, jnp.concatenate(halves(value), axis=1))
    return both[:, 0:LANES] + both[:, LANES : 2 * LANES]


def iota(shape, axis):
    return lax.broadcasted_iota(jnp.int32, shape, axis).astype(F32)


def column_of(row_vector):
    n = row_vector.shape[1]
    return jnp.sum(
        jnp.where(iota((n, n), 0) == iota((n, n), 1), row_vector, 0.0), axis=1, keepdims=True
    )


def fold(value):
    return jnp.sum(value, axis=0, keepdims=True)


def total_of(value):
    return jnp.sum(value, axis=(0, 1), keepdims=True)


def spread_row(row):
    tile = jnp.broadcast_to(row, (16, TRACKS)).astype(BF16)
    return jnp.concatenate([tile] * 8, axis=0)


def block_terms(jac0, jac1, rad, resid, damp):
    h0, h1 = rad[0:1, :], rad[1:2, :]
    e0, e1 = resid[0:1, :], resid[1:2, :]
    inverse = 1.0 / (h0 * h0 + h1 * h1 + damp)
    grad = (h0 * e0 + h1 * e1) * inverse
    coef0 = spread_row(1.0 - h0 * h0 * inverse)
    coef1 = spread_row(1.0 - h1 * h1 * inverse)
    coef2 = spread_row(-h0 * h1 * inverse)
    coef3 = jnp.broadcast_to(e0 - h0 * grad, (16, TRACKS)).astype(BF16)
    coef4 = jnp.broadcast_to(e1 - h1 * grad, (16, TRACKS)).astype(BF16)
    jac0_t, jac1_t = jac0.T, jac1.T
    first = dot(jnp.concatenate([coef0 * jac0_t, coef3], axis=0), jac0)
    second = dot(jnp.concatenate([coef1 * jac1_t, coef4], axis=0), jac1)
    first, second = first.astype(BF16), second.astype(BF16)
    block_a, vector_a = first[0:128], first[128:144]
    block_b, vector_b = second[0:128], second[128:144]
    eye = iota((LANES, LANES), 0) == iota((LANES, LANES), 1)
    diag_a = fold(jnp.where(eye, block_a.astype(F32), 0.0))
    diag_b = fold(jnp.where(eye, block_b.astype(F32), 0.0))
    terms_a = jnp.concatenate([vector_a.astype(F32)[0:1], diag_a], axis=1)
    terms_b = jnp.concatenate([vector_b.astype(F32)[0:1], diag_b], axis=1)
    return block_a, block_b, coef2 * jac1_t, terms_a, terms_b


def kernel(
    jac_hbm,
    rad_hbm,
    resid_hbm,
    track_hbm,
    damp_ref,
    column_ref,
    slot_ref,
    rows_ref,
    cols_ref,
    state_ref,
    jac_ref,
    rad_ref,
    resid_ref,
    track_ref,
    weight_a,
    weight_b,
    weight_c,
    cross_ref,
    terms_a,
    terms_b,
    index_src,
    index_buf,
    rhs_b_src,
    rhs_b_buf,
    rhs_a_src,
    rhs_a_buf,
    rhs_r_src,
    rhs_r_buf,
    near_src,
    near_buf,
    field_src,
    field_buf,
    pick_src,
    pick_buf,
    prod_src,
    prod_buf,
    part_a_src,
    part_a_buf,
    part_b_src,
    part_b_buf,
    left_buf,
    send_hot,
    take_hot,
    pick_a,
    place_a,
    pick_b,
    place_b,
    vector_ref,
    rows_state,
    scalar_ref,
    load_sem,
    jac_sem,
    send_sem,
    recv_sem,
):
    row, col = lax.axis_index("row"), lax.axis_index("col")

    small = [
        pltpu.make_async_copy(src, dst, load_sem.at[i])
        for i, (src, dst) in enumerate(
            [(rad_hbm, rad_ref), (resid_hbm, resid_ref), (track_hbm, track_ref)]
        )
    ]
    for copy in small:
        copy.start()

    def load(step):
        part = pl.ds(step * STEP, STEP)
        return pltpu.make_async_copy(jac_hbm.at[part], jac_ref.at[part], jac_sem.at[step])

    def start_load(step, carry):
        load(step).start()
        return carry

    lax.fori_loop(0, AHEAD, start_load, 0)

    for ref in (index_buf, rhs_b_buf, pick_buf, prod_buf):
        ref[...] = jnp.zeros_like(ref)

    barrier = pltpu.get_barrier_semaphore()

    col_hi, col_lo = lax.div(col, 4), lax.rem(col, 4)
    row_hi, row_lo = lax.div(row, 2), lax.rem(row, 2)
    col_steps = sorted(
        [(i, j) for i in range(4) for j in range(4) if i or j],
        key=lambda step: -sum(min(d, 4 - d) for d in step),
    )
    row_steps = [(i, j) for i in (2, 1, 3, 0) for j in (1, 0) if i or j]
    col_peers = [lax.rem(col_hi + i, 4) * 4 + lax.rem(col_lo + j, 4) for i, j in col_steps]
    row_peers = [lax.rem(row_hi + i, 4) * 2 + lax.rem(row_lo + j, 2) for i, j in row_steps]

    for peer in col_peers:
        pl.semaphore_signal(barrier, inc=1, device_id=(row, peer), device_id_type=MESH)
    for peer in row_peers:
        pl.semaphore_signal(barrier, inc=1, device_id=(peer, col), device_id_type=MESH)

    def send(phase, source, target, over_col, rows):
        peers, me = (col_peers, col) if over_col else (row_peers, row)
        for peer in peers:
            pltpu.make_async_remote_copy(
                src_ref=source(peer).at[pl.ds(0, rows)],
                dst_ref=target.at[me, pl.ds(0, rows)],
                send_sem=send_sem.at[phase],
                recv_sem=recv_sem.at[phase],
                device_id=(row, peer) if over_col else (peer, col),
                device_id_type=MESH,
            ).start()

    def waiter(phase, target, over_col, rows):
        peers = col_peers if over_col else row_peers
        whole = target.at[pl.ds(0, len(peers)), pl.ds(0, rows)]
        return pltpu.make_async_remote_copy(
            src_ref=whole,
            dst_ref=whole,
            send_sem=send_sem.at[phase],
            recv_sem=recv_sem.at[phase],
            device_id=(row, peers[0]) if over_col else (peers[0], col),
            device_id_type=MESH,
        )

    def form(step, carry):
        pl.when(step == 4)(send_index)
        pl.when(step == 12)(read_index)
        pl.when(step + AHEAD < BLOCKS // STEP)(lambda: load(step + AHEAD).start())
        load(step).wait()
        blocks = [step * STEP + i for i in range(STEP)]
        formed = [
            block_terms(
                jac_ref[k, 0], jac_ref[k, 1], rad_ref[k], resid_ref[k], track_ref[pl.ds(k, 1), :]
            )
            for k in blocks
        ]
        for k, (block_a, block_b, cross, row_a, row_b) in zip(blocks, formed):
            at = pl.ds(pl.multiple_of(k * LANES, LANES), LANES)
            weight_a[at, 0:LANES] = block_a
            weight_b[at, :] = block_b
            cross_ref[k] = cross
            terms_a[pl.ds(k, 1), :] = row_a
            terms_b[pl.ds(k, 1), :] = row_b
        return carry

    def form_cross(first, last):
        def one(step, carry):
            blocks = [step * 4 + i for i in range(4)]
            formed = [dot(cross_ref[k], jac_ref[k, 0]).astype(BF16) for k in blocks]
            formed = [(block_c, block_c.T) for block_c in formed]
            for k, (block_c, block_c_t) in zip(blocks, formed):
                at = pl.ds(pl.multiple_of(k * LANES, LANES), LANES)
                weight_c[at, :] = block_c
                weight_a[at, LANES : 2 * LANES] = block_c_t
            return carry

        lax.fori_loop(first // 4, last // 4, one, 0)

    def block_columns():
        column_row = column_ref[...].astype(F32)
        column = column_of(column_row)
        same = jnp.logical_and(
            column == column_row, iota((BLOCKS, BLOCKS), 1) < iota((BLOCKS, BLOCKS), 0)
        )
        return column, column * SLOT + jnp.sum(jnp.where(same, 1.0, 0.0), axis=1, keepdims=True)

    def send_index():
        column, place_col = block_columns()
        place_row = fold(
            jnp.where(iota((BLOCKS, BLOCKS), 0) == iota((BLOCKS, BLOCKS), 1), place_col, 0.0)
        )
        send_true = iota((SLOTS, BLOCKS), 0) == place_row
        send_hot[...] = jnp.where(send_true, 1.0, 0.0).astype(BF16)
        take_hot[...] = jnp.where(iota((BLOCKS, SLOTS), 1) == place_col, 1.0, 0.0).astype(BF16)
        slot_row = slot_ref[...].astype(F32)
        slots_out = jnp.sum(jnp.where(send_true, slot_row + 1.0, 0.0), axis=1, keepdims=True) - 1.0
        index_src[...] = jnp.broadcast_to(slots_out, (SLOTS, LANES)).reshape(N_COL, SLOT, LANES)
        for j in range(N_COL):
            index_src[j, CAP : CAP + 1, 0:BLOCKS] = rows_ref[...].astype(F32)
        index_buf[col] = index_src[col]
        pl.semaphore_wait(barrier, N_COL + N_ROW - 2)
        send(0, lambda peer: index_src.at[peer], index_buf, True, SENT)

    def read_index():
        waiter(0, index_buf, True, SENT).wait_recv()
        column, _ = block_columns()
        picked = iota((BLOCKS, LANES), 1) == column_of(slot_ref[...].astype(F32))
        names_a = jnp.zeros((BLOCKS, LANES), F32)
        for j in range(N_COL):
            names_a = names_a + jnp.where(column == float(j), index_buf[j, CAP : CAP + 1, :], 0.0)
        key_a = jnp.sum(jnp.where(picked, names_a, 0.0), axis=1, keepdims=True)
        pick = jnp.where(iota((BLOCKS, IMG_ROW), 1) == key_a, 1.0, 0.0)
        pick_a[...] = pick.astype(BF16)
        pick = jnp.concatenate([pick, jnp.zeros((LANES - BLOCKS, IMG_ROW), F32)], axis=0)
        place_a[...] = pick.T.astype(BF16)
        slots_in = index_buf[...].reshape(SLOTS, LANES)
        used = jnp.logical_and(lax.rem(slot_sub, SLOT) < CAP, slots_in == iota((SLOTS, LANES), 1))
        cols_row = jnp.concatenate(
            [cols_ref[...].astype(F32), jnp.zeros((1, LANES - BLOCKS), F32)], axis=1
        )
        key_b = jnp.sum(jnp.where(used, cols_row + 1.0, 0.0), axis=1, keepdims=True) - 1.0
        pick = jnp.where(iota((SLOTS, LANES), 1) == key_b, 1.0, 0.0)
        pick_b[...] = pick.astype(BF16)
        place_b[...] = pick.T.astype(BF16)

    slot_sub = lax.broadcasted_iota(jnp.int32, (SLOTS, LANES), 0)
    scalar_rows = lax.rem(slot_sub, SLOT) == CAP
    for copy in small:
        copy.wait()
    lax.fori_loop(0, BLOCKS // STEP, form, 0)

    damping = damp_ref[...]
    pad_a = jnp.zeros((LANES - BLOCKS, 256), BF16)

    rhs_b_src[...] = dot(send_hot[...], terms_b[...].astype(BF16)).reshape(N_COL, SLOT, 256)
    rhs_b_buf[col] = rhs_b_src[col]
    send(1, lambda peer: rhs_b_src.at[peer], rhs_b_buf, True, SENT)
    rhs_a_src[...] = dot(
        place_a[...], jnp.concatenate([terms_a[...].astype(BF16), pad_a], axis=0)
    ).reshape(N_COL, IMG, 256)
    rhs_a_buf[col] = rhs_a_src[col]
    send(2, lambda peer: rhs_a_src.at[peer], rhs_a_buf, True, IMG)
    form_cross(0, 12)
    waiter(1, rhs_b_buf, True, SENT).wait_recv()
    rhs_r_src[...] = dot(place_b[...], rhs_b_buf[...].reshape(SLOTS, 256).astype(BF16)).reshape(
        N_ROW, IMG, 256
    )
    rhs_r_buf[row] = rhs_r_src[row]
    send(3, lambda peer: rhs_r_src.at[peer], rhs_r_buf, False, IMG)
    form_cross(12, 24)
    waiter(2, rhs_a_buf, True, IMG).wait_recv()
    sums = jnp.sum(rhs_a_buf[...], axis=0)
    for sent in (
        (0, index_buf, True, SENT),
        (1, rhs_b_buf, True, SENT),
        (2, rhs_a_buf, True, IMG),
    ):
        waiter(*sent).wait_send()
    waiter(3, rhs_r_buf, False, IMG).wait_recv()
    sums = sums + jnp.sum(rhs_r_buf[...], axis=0)
    right_side = sums[:, 0:LANES]
    diagonal = damping + sums[:, LANES:256]

    row_in_left = lax.broadcasted_iota(jnp.int32, (2 * BLOCKS, LANES), 0)

    def spread(value, slot):
        stacked = jnp.concatenate(halves(value), axis=0)
        for k in range(BLOCKS):
            keep = jnp.logical_or(row_in_left == k, row_in_left == k + BLOCKS)
            left_buf[slot, :, k * LANES : (k + 1) * LANES] = jnp.where(
                keep, stacked, jnp.zeros_like(stacked)
            )

    def products(slot, weight):
        both = dot(left_buf[slot], weight[...])
        return both[0:BLOCKS] + both[BLOCKS : 2 * BLOCKS]

    def exchanges(t):
        return [
            (4 + 6 * t, near_buf.at[t], False, IMG + 1),
            (5 + 6 * t, field_buf.at[t], True, IMG),
            (6 + 6 * t, pick_buf.at[t], True, SENT),
            (7 + 6 * t, prod_buf.at[t], True, SENT),
            (8 + 6 * t, part_a_buf.at[t], True, IMG),
            (9 + 6 * t, part_b_buf.at[t], False, IMG + 1),
        ]

    def iteration(t, carry):
        update, own, residual, image = (vector_ref[i] for i in range(4))
        dir_a, dir_b, *prods = (rows_state[i] for i in range(6))
        step_length, inner_now = scalar_ref[0, 0:1, :], scalar_ref[1, 0:1, :]
        near, field, pick, prod, part_a, part_b = exchanges(t)
        update = update + step_length * own
        residual = residual - step_length * image
        scaled = residual / diagonal
        near_src[t, 0:IMG, :] = scaled
        near_src[t, IMG : IMG + 1, :] = fold(residual * scaled)
        near_buf[t, row] = near_src[t]
        send(near[0], lambda peer: near_src.at[t], *near[1:])
        field_src[t] = scaled
        field_buf[t, col] = scaled
        send(field[0], lambda peer: field_src.at[t], *field[1:])
        pl.when(t == 0)(lambda: form_cross(24, 32))

        waiter(*near).wait_recv()
        picks = hot_dot(pick_b[...], near_buf[t, :, 0:IMG, :].reshape(IMG_COL, LANES))
        norm = total_of(jnp.sum(near_buf[t, :, IMG : IMG + 1, :], axis=0))
        pick_src[t] = jnp.where(scalar_rows, norm, picks).reshape(N_COL, SLOT, LANES)
        pick_buf[t, col] = pick_src[t, col]
        send(pick[0], lambda peer: pick_src.at[t, peer], *pick[1:])

        waiter(*field).wait_recv()
        field_a = hot_dot(pick_a[...], field_buf[t].reshape(IMG_ROW, LANES))
        spread(field_a, 0)
        from_a = products(0, weight_a)

        waiter(*pick).wait_recv()
        received = pick_buf[t].reshape(SLOTS, LANES)
        field_b = hot_dot(take_hot[...], received)
        spread(field_b, 1)
        from_b = products(1, weight_b)
        inner_next = fold(jnp.where(scalar_rows, received, 0.0))
        ratio = jnp.where(t == 0, 0.0, inner_next / inner_now)
        own = scaled + ratio * own
        dir_a = field_a + ratio * dir_a
        dir_b = field_b + ratio * dir_b
        prod_aa, prod_ca, prod_bb, prod_cb = prods
        prod_aa = from_a[:, 0:LANES] + ratio * prod_aa
        prod_ca = from_a[:, LANES:256] + ratio * prod_ca
        prod_bb = from_b + ratio * prod_bb
        step_row = total_of(
            fold(dir_a * prod_aa + dir_b * (2.0 * prod_ca + prod_bb)) + fold(damping * own * own)
        )
        sent = hot_dot(send_hot[...], prod_ca + prod_bb)
        prod_src[t] = jnp.where(scalar_rows, step_row, sent).reshape(N_COL, SLOT, LANES)
        prod_buf[t, col] = prod_src[t, col]
        send(prod[0], lambda peer: prod_src.at[t, peer], *prod[1:])

        prod_cb = products(1, weight_c) + ratio * prod_cb
        part = hot_dot(
            place_a[...],
            jnp.concatenate([prod_aa + prod_cb, jnp.zeros((LANES - BLOCKS, LANES), F32)], axis=0),
        )
        part_a_src[t] = part.reshape(N_COL, IMG, LANES)
        part_a_buf[t, col] = part_a_src[t, col]
        send(part_a[0], lambda peer: part_a_src.at[t, peer], *part_a[1:])

        waiter(*prod).wait_recv()
        received = prod_buf[t].reshape(SLOTS, LANES)
        part = hot_dot(place_b[...], received)
        part_b_src[t, :, 0:IMG, :] = part.reshape(N_ROW, IMG, LANES)
        step_row = fold(jnp.where(scalar_rows, received, 0.0))
        part_b_src[t, :, IMG : IMG + 1, :] = jnp.broadcast_to(step_row, (N_ROW, 1, LANES))
        part_b_buf[t, row] = part_b_src[t, row]
        send(part_b[0], lambda peer: part_b_src.at[t, peer], *part_b[1:])

        waiter(*part_a).wait_recv()
        image = damping * own + jnp.sum(part_a_buf[t], axis=0)
        for sent in (near, field, pick, prod, part_a):
            waiter(*sent).wait_send()
        waiter(*part_b).wait_recv()
        sums = jnp.sum(part_b_buf[t, :, 0 : IMG + 1, :], axis=0)
        image = image + sums[0:IMG]
        step_length = inner_next / sums[IMG : IMG + 1]
        for i, value in enumerate([update, own, residual, image]):
            vector_ref[i] = value
        for i, value in enumerate([dir_a, dir_b, prod_aa, prod_ca, prod_bb, prod_cb]):
            rows_state[i] = value
        scalar_ref[0] = jnp.broadcast_to(step_length, (8, LANES))
        scalar_ref[1] = jnp.broadcast_to(inner_next, (8, LANES))
        return carry

    vector_ref[...] = jnp.zeros_like(vector_ref)
    vector_ref[2] = right_side
    rows_state[...] = jnp.zeros_like(rows_state)
    scalar_ref[0] = jnp.zeros((8, LANES), F32)
    scalar_ref[1] = jnp.ones((8, LANES), F32)
    lax.fori_loop(0, ITERS, iteration, 0)
    state_ref[0:4] = vector_ref[...]
    state_ref[4] = jnp.broadcast_to(scalar_ref[0, 0:1, :], (IMG, LANES))

    waiter(3, rhs_r_buf, False, IMG).wait_send()

    def drain(t, carry):
        waiter(*exchanges(t)[-1]).wait_send()
        return carry

    lax.fori_loop(0, ITERS, drain, 0)


def shards(
    obs_jac,
    rad_jac,
    obs_residual,
    track_damping,
    track_block_column,
    track_slot,
    pair_rows,
    pair_cols,
    image_damping,
):

    def both(*shape, dtype=F32):
        return [pltpu.VMEM(shape, dtype)] * 2

    scratch = [
        pltpu.VMEM(obs_jac.shape, BF16),
        pltpu.VMEM(rad_jac.shape, F32),
        pltpu.VMEM(obs_residual.shape, F32),
        pltpu.VMEM(track_damping.shape, F32),
        pltpu.VMEM((BLOCKS * LANES, 256), BF16),
        *both(BLOCKS * LANES, LANES, dtype=BF16),
        pltpu.VMEM((BLOCKS, LANES, TRACKS), BF16),
        *both(BLOCKS, 256),
        *both(N_COL, SLOT, LANES),
        *both(N_COL, SLOT, 256),
        *both(N_COL, IMG, 256),
        *both(N_ROW, IMG, 256),
        pltpu.VMEM((ITERS, IMG + 8, LANES), F32),
        pltpu.VMEM((ITERS, N_ROW, IMG + 8, LANES), F32),
        pltpu.VMEM((ITERS, IMG, LANES), F32),
        pltpu.VMEM((ITERS, N_COL, IMG, LANES), F32),
        *both(ITERS, N_COL, SLOT, LANES),
        *both(ITERS, N_COL, SLOT, LANES),
        *both(ITERS, N_COL, IMG, LANES),
        *both(ITERS, N_ROW, IMG + 8, LANES),
        pltpu.VMEM((2, 2 * BLOCKS, BLOCKS * LANES), BF16),
        pltpu.VMEM((SLOTS, BLOCKS), BF16),
        pltpu.VMEM((BLOCKS, SLOTS), BF16),
        pltpu.VMEM((BLOCKS, IMG_ROW), BF16),
        pltpu.VMEM((IMG_ROW, LANES), BF16),
        *both(SLOTS, LANES, dtype=BF16),
        pltpu.VMEM((4, IMG, LANES), F32),
        pltpu.VMEM((6, BLOCKS, LANES), F32),
        pltpu.VMEM((2, 8, LANES), F32),
        pltpu.SemaphoreType.DMA((3,)),
        pltpu.SemaphoreType.DMA((BLOCKS // STEP,)),
        pltpu.SemaphoreType.DMA((PHASES,)),
        pltpu.SemaphoreType.DMA((PHASES,)),
    ]
    hbm = pl.BlockSpec(memory_space=pltpu.HBM)
    vmem = pl.BlockSpec(memory_space=pltpu.VMEM)
    state = (
        pl.pallas_call(
            kernel,
            out_shape=jax.ShapeDtypeStruct((5, IMG, LANES), F32),
            in_specs=[hbm] * 4 + [vmem] * 5,
            out_specs=vmem,
            scratch_shapes=scratch,
            compiler_params=pltpu.CompilerParams(
                collective_id=0, has_side_effects=True, vmem_limit_bytes=56 * 1024 * 1024
            ),
        )(
            obs_jac,
            rad_jac,
            obs_residual,
            track_damping,
            image_damping,
            track_block_column.reshape(1, BLOCKS),
            track_slot.reshape(1, BLOCKS),
            pair_rows.reshape(1, BLOCKS),
            pair_cols.reshape(1, BLOCKS),
        )
    )
    return state[0] + state[4] * state[1], state[2] - state[4] * state[3]


def solution(mesh):
    in_specs = (
        P(("row", "col"), None, None, None),
        P(("row", "col"), None, None),
        P(("row", "col"), None, None),
        P(("row", "col"), None),
        P(("row", "col"), None),
        P(("row", "col")),
        P(("row", "col")),
        P(("row", "col")),
        P(("row", "col"), None),
    )
    out_specs = (P(("row", "col"), None), P(("row", "col"), None))
    return jax.shard_map(shards, mesh=mesh, in_specs=in_specs, out_specs=out_specs, check_vma=False)
```

```python
import jax
import jax.numpy as jnp
from jax import lax
from jax.experimental import pallas as pl
from jax.experimental.pallas import tpu as pltpu
from jax.sharding import PartitionSpec as P

ITERS = 3
N_ROW = 8
N_COL = 16
BLOCKS = 32
IMG = 16
IMG_ROW = N_COL * IMG
IMG_COL = N_ROW * IMG
LANES = 128
TRACKS = 1024
STEP = 4
CAP = 3
AHEAD = 4
SLOT = 8
SENT = 4
SLOTS = N_COL * SLOT
PHASES = 3 + 1 + 6 * ITERS
MESH = pl.DeviceIdType.MESH
F32 = jnp.float32
BF16 = jnp.bfloat16


def dot(left, right):
    return jnp.dot(left, right, preferred_element_type=F32)


def halves(value):
    high = value.astype(BF16)
    low = (value - high.astype(F32)).astype(BF16)
    return high, low


def hot_dot(hot, value):
    both = dot(hot, jnp.concatenate(halves(value), axis=1))
    return both[:, 0:LANES] + both[:, LANES : 2 * LANES]


def iota(shape, axis):
    return lax.broadcasted_iota(jnp.int32, shape, axis).astype(F32)


def column_of(row_vector):
    n = row_vector.shape[1]
    return jnp.sum(
        jnp.where(iota((n, n), 0) == iota((n, n), 1), row_vector, 0.0), axis=1, keepdims=True
    )


def fold(value):
    return jnp.sum(value, axis=0, keepdims=True)


def total_of(value):
    return jnp.sum(value, axis=(0, 1), keepdims=True)


def spread_row(row):
    tile = jnp.broadcast_to(row, (16, TRACKS)).astype(BF16)
    return jnp.concatenate([tile] * 8, axis=0)


def block_terms(jac0, jac1, rad, resid, damp):
    h0, h1 = rad[0:1, :], rad[1:2, :]
    e0, e1 = resid[0:1, :], resid[1:2, :]
    inverse = 1.0 / (h0 * h0 + h1 * h1 + damp)
    grad = (h0 * e0 + h1 * e1) * inverse
    coef0 = spread_row(1.0 - h0 * h0 * inverse)
    coef1 = spread_row(1.0 - h1 * h1 * inverse)
    coef2 = spread_row(-h0 * h1 * inverse)
    coef3 = jnp.broadcast_to(e0 - h0 * grad, (16, TRACKS)).astype(BF16)
    coef4 = jnp.broadcast_to(e1 - h1 * grad, (16, TRACKS)).astype(BF16)
    jac0_t, jac1_t = jac0.T, jac1.T
    first = dot(jnp.concatenate([coef0 * jac0_t, coef3], axis=0), jac0)
    second = dot(jnp.concatenate([coef1 * jac1_t, coef4], axis=0), jac1)
    first, second = first.astype(BF16), second.astype(BF16)
    block_a, vector_a = first[0:128], first[128:144]
    block_b, vector_b = second[0:128], second[128:144]
    eye = iota((LANES, LANES), 0) == iota((LANES, LANES), 1)
    diag_a = fold(jnp.where(eye, block_a.astype(F32), 0.0))
    diag_b = fold(jnp.where(eye, block_b.astype(F32), 0.0))
    terms_a = jnp.concatenate([vector_a.astype(F32)[0:1], diag_a], axis=1)
    terms_b = jnp.concatenate([vector_b.astype(F32)[0:1], diag_b], axis=1)
    return block_a, block_b, coef2 * jac1_t, terms_a, terms_b


def kernel(
    jac_hbm,
    rad_hbm,
    resid_hbm,
    track_hbm,
    damp_ref,
    column_ref,
    slot_ref,
    rows_ref,
    cols_ref,
    state_ref,
    jac_ref,
    rad_ref,
    resid_ref,
    track_ref,
    weight_a,
    weight_b,
    weight_c,
    cross_ref,
    terms_a,
    terms_b,
    index_src,
    index_buf,
    rhs_b_src,
    rhs_b_buf,
    rhs_a_src,
    rhs_a_buf,
    rhs_r_src,
    rhs_r_buf,
    near_src,
    near_buf,
    field_src,
    field_buf,
    pick_src,
    pick_buf,
    prod_src,
    prod_buf,
    part_a_src,
    part_a_buf,
    part_b_src,
    part_b_buf,
    left_buf,
    send_hot,
    take_hot,
    pick_a,
    place_a,
    pick_b,
    place_b,
    vector_ref,
    rows_state,
    scalar_ref,
    load_sem,
    jac_sem,
    send_sem,
    recv_sem,
):
    row, col = lax.axis_index("row"), lax.axis_index("col")

    small = [
        pltpu.make_async_copy(src, dst, load_sem.at[i])
        for i, (src, dst) in enumerate(
            [(rad_hbm, rad_ref), (resid_hbm, resid_ref), (track_hbm, track_ref)]
        )
    ]
    for copy in small:
        copy.start()

    def load(step):
        part = pl.ds(step * STEP, STEP)
        return pltpu.make_async_copy(jac_hbm.at[part], jac_ref.at[part], jac_sem.at[step])

    def start_load(step, carry):
        load(step).start()
        return carry

    lax.fori_loop(0, AHEAD, start_load, 0)

    for ref in (index_buf, rhs_b_buf, pick_buf, prod_buf):
        ref[...] = jnp.zeros_like(ref)

    barrier = pltpu.get_barrier_semaphore()

    col_hi, col_lo = lax.div(col, 4), lax.rem(col, 4)
    row_hi, row_lo = lax.div(row, 2), lax.rem(row, 2)
    col_steps = sorted(
        [(i, j) for i in range(4) for j in range(4) if i or j],
        key=lambda step: -sum(min(d, 4 - d) for d in step),
    )
    row_steps = [(i, j) for i in (2, 1, 3, 0) for j in (1, 0) if i or j]
    col_peers = [lax.rem(col_hi + i, 4) * 4 + lax.rem(col_lo + j, 4) for i, j in col_steps]
    row_peers = [lax.rem(row_hi + i, 4) * 2 + lax.rem(row_lo + j, 2) for i, j in row_steps]

    for peer in col_peers:
        pl.semaphore_signal(barrier, inc=1, device_id=(row, peer), device_id_type=MESH)
    for peer in row_peers:
        pl.semaphore_signal(barrier, inc=1, device_id=(peer, col), device_id_type=MESH)

    def send(phase, source, target, over_col, rows):
        peers, me = (col_peers, col) if over_col else (row_peers, row)
        for peer in peers:
            pltpu.make_async_remote_copy(
                src_ref=source(peer).at[pl.ds(0, rows)],
                dst_ref=target.at[me, pl.ds(0, rows)],
                send_sem=send_sem.at[phase],
                recv_sem=recv_sem.at[phase],
                device_id=(row, peer) if over_col else (peer, col),
                device_id_type=MESH,
            ).start()

    def waiter(phase, target, over_col, rows):
        peers = col_peers if over_col else row_peers
        whole = target.at[pl.ds(0, len(peers)), pl.ds(0, rows)]
        return pltpu.make_async_remote_copy(
            src_ref=whole,
            dst_ref=whole,
            send_sem=send_sem.at[phase],
            recv_sem=recv_sem.at[phase],
            device_id=(row, peers[0]) if over_col else (peers[0], col),
            device_id_type=MESH,
        )

    def form(step, carry):
        pl.when(step == 2)(send_index)
        pl.when(step == 6)(read_index)
        pl.when(step + AHEAD < BLOCKS // STEP)(lambda: load(step + AHEAD).start())
        load(step).wait()
        blocks = [step * STEP + i for i in range(STEP)]
        formed = [
            block_terms(
                jac_ref[k, 0], jac_ref[k, 1], rad_ref[k], resid_ref[k], track_ref[pl.ds(k, 1), :]
            )
            for k in blocks
        ]
        for k, (block_a, block_b, cross, row_a, row_b) in zip(blocks, formed):
            at = pl.ds(pl.multiple_of(k * LANES, LANES), LANES)
            weight_a[at, 0:LANES] = block_a
            weight_b[at, :] = block_b
            cross_ref[k] = cross
            terms_a[pl.ds(k, 1), :] = row_a
            terms_b[pl.ds(k, 1), :] = row_b
        return carry

    def form_cross(first, last):
        def one(step, carry):
            blocks = [step * 4 + i for i in range(4)]
            formed = [dot(cross_ref[k], jac_ref[k, 0]).astype(BF16) for k in blocks]
            formed = [(block_c, block_c.T) for block_c in formed]
            for k, (block_c, block_c_t) in zip(blocks, formed):
                at = pl.ds(pl.multiple_of(k * LANES, LANES), LANES)
                weight_c[at, :] = block_c
                weight_a[at, LANES : 2 * LANES] = block_c_t
            return carry

        lax.fori_loop(first // 4, last // 4, one, 0)

    def block_columns():
        column_row = column_ref[...].astype(F32)
        column = column_of(column_row)
        same = jnp.logical_and(
            column == column_row, iota((BLOCKS, BLOCKS), 1) < iota((BLOCKS, BLOCKS), 0)
        )
        return column, column * SLOT + jnp.sum(jnp.where(same, 1.0, 0.0), axis=1, keepdims=True)

    def send_index():
        column, place_col = block_columns()
        place_row = fold(
            jnp.where(iota((BLOCKS, BLOCKS), 0) == iota((BLOCKS, BLOCKS), 1), place_col, 0.0)
        )
        send_true = iota((SLOTS, BLOCKS), 0) == place_row
        send_hot[...] = jnp.where(send_true, 1.0, 0.0).astype(BF16)
        take_hot[...] = jnp.where(iota((BLOCKS, SLOTS), 1) == place_col, 1.0, 0.0).astype(BF16)
        slot_row = slot_ref[...].astype(F32)
        slots_out = jnp.sum(jnp.where(send_true, slot_row + 1.0, 0.0), axis=1, keepdims=True) - 1.0
        index_src[...] = jnp.broadcast_to(slots_out, (SLOTS, LANES)).reshape(N_COL, SLOT, LANES)
        for j in range(N_COL):
            index_src[j, CAP : CAP + 1, 0:BLOCKS] = rows_ref[...].astype(F32)
        index_buf[col] = index_src[col]
        pl.semaphore_wait(barrier, N_COL + N_ROW - 2)
        send(0, lambda peer: index_src.at[peer], index_buf, True, SENT)

    def read_index():
        waiter(0, index_buf, True, SENT).wait_recv()
        column, _ = block_columns()
        picked = iota((BLOCKS, LANES), 1) == column_of(slot_ref[...].astype(F32))
        names_a = jnp.zeros((BLOCKS, LANES), F32)
        for j in range(N_COL):
            names_a = names_a + jnp.where(column == float(j), index_buf[j, CAP : CAP + 1, :], 0.0)
        key_a = jnp.sum(jnp.where(picked, names_a, 0.0), axis=1, keepdims=True)
        pick = jnp.where(iota((BLOCKS, IMG_ROW), 1) == key_a, 1.0, 0.0)
        pick_a[...] = pick.astype(BF16)
        pick = jnp.concatenate([pick, jnp.zeros((LANES - BLOCKS, IMG_ROW), F32)], axis=0)
        place_a[...] = pick.T.astype(BF16)
        slots_in = index_buf[...].reshape(SLOTS, LANES)
        used = jnp.logical_and(lax.rem(slot_sub, SLOT) < CAP, slots_in == iota((SLOTS, LANES), 1))
        cols_row = jnp.concatenate(
            [cols_ref[...].astype(F32), jnp.zeros((1, LANES - BLOCKS), F32)], axis=1
        )
        key_b = jnp.sum(jnp.where(used, cols_row + 1.0, 0.0), axis=1, keepdims=True) - 1.0
        pick = jnp.where(iota((SLOTS, LANES), 1) == key_b, 1.0, 0.0)
        pick_b[...] = pick.astype(BF16)
        place_b[...] = pick.T.astype(BF16)

    slot_sub = lax.broadcasted_iota(jnp.int32, (SLOTS, LANES), 0)
    scalar_rows = lax.rem(slot_sub, SLOT) == CAP
    for copy in small:
        copy.wait()
    lax.fori_loop(0, BLOCKS // STEP, form, 0)

    damping = damp_ref[...]
    pad_a = jnp.zeros((LANES - BLOCKS, 256), BF16)

    rhs_b_src[...] = dot(send_hot[...], terms_b[...].astype(BF16)).reshape(N_COL, SLOT, 256)
    rhs_b_buf[col] = rhs_b_src[col]
    send(1, lambda peer: rhs_b_src.at[peer], rhs_b_buf, True, SENT)
    rhs_a_src[...] = dot(
        place_a[...], jnp.concatenate([terms_a[...].astype(BF16), pad_a], axis=0)
    ).reshape(N_COL, IMG, 256)
    rhs_a_buf[col] = rhs_a_src[col]
    send(2, lambda peer: rhs_a_src.at[peer], rhs_a_buf, True, IMG)
    form_cross(0, 8)
    waiter(1, rhs_b_buf, True, SENT).wait_recv()
    rhs_r_src[...] = dot(place_b[...], rhs_b_buf[...].reshape(SLOTS, 256).astype(BF16)).reshape(
        N_ROW, IMG, 256
    )
    rhs_r_buf[row] = rhs_r_src[row]
    send(3, lambda peer: rhs_r_src.at[peer], rhs_r_buf, False, IMG)
    form_cross(8, 16)
    waiter(2, rhs_a_buf, True, IMG).wait_recv()
    sums = jnp.sum(rhs_a_buf[...], axis=0)
    for sent in (
        (0, index_buf, True, SENT),
        (1, rhs_b_buf, True, SENT),
        (2, rhs_a_buf, True, IMG),
    ):
        waiter(*sent).wait_send()
    waiter(3, rhs_r_buf, False, IMG).wait_recv()
    sums = sums + jnp.sum(rhs_r_buf[...], axis=0)
    right_side = sums[:, 0:LANES]
    diagonal = damping + sums[:, LANES:256]

    row_in_left = lax.broadcasted_iota(jnp.int32, (2 * BLOCKS, LANES), 0)

    def spread(value, slot):
        stacked = jnp.concatenate(halves(value), axis=0)
        for k in range(BLOCKS):
            keep = jnp.logical_or(row_in_left == k, row_in_left == k + BLOCKS)
            left_buf[slot, :, k * LANES : (k + 1) * LANES] = jnp.where(
                keep, stacked, jnp.zeros_like(stacked)
            )

    def products(slot, weight):
        both = dot(left_buf[slot], weight[...])
        return both[0:BLOCKS] + both[BLOCKS : 2 * BLOCKS]

    def exchanges(t):
        return [
            (4 + 6 * t, near_buf.at[t], False, IMG + 1),
            (5 + 6 * t, field_buf.at[t], True, IMG),
            (6 + 6 * t, pick_buf.at[t], True, SENT),
            (7 + 6 * t, prod_buf.at[t], True, SENT),
            (8 + 6 * t, part_a_buf.at[t], True, IMG),
            (9 + 6 * t, part_b_buf.at[t], False, IMG + 1),
        ]

    def iteration(t, carry):
        update, own, residual, image = (vector_ref[i] for i in range(4))
        dir_a, dir_b, *prods = (rows_state[i] for i in range(6))
        step_length, inner_now = scalar_ref[0, 0:1, :], scalar_ref[1, 0:1, :]
        near, field, pick, prod, part_a, part_b = exchanges(t)
        update = update + step_length * own
        residual = residual - step_length * image
        scaled = residual / diagonal
        near_src[t, 0:IMG, :] = scaled
        near_src[t, IMG : IMG + 1, :] = fold(residual * scaled)
        near_buf[t, row] = near_src[t]
        send(near[0], lambda peer: near_src.at[t], *near[1:])
        field_src[t] = scaled
        field_buf[t, col] = scaled
        send(field[0], lambda peer: field_src.at[t], *field[1:])
        pl.when(t == 0)(lambda: form_cross(16, 24))

        waiter(*near).wait_recv()
        picks = hot_dot(pick_b[...], near_buf[t, :, 0:IMG, :].reshape(IMG_COL, LANES))
        norm = total_of(jnp.sum(near_buf[t, :, IMG : IMG + 1, :], axis=0))
        pick_src[t] = jnp.where(scalar_rows, norm, picks).reshape(N_COL, SLOT, LANES)
        pick_buf[t, col] = pick_src[t, col]
        send(pick[0], lambda peer: pick_src.at[t, peer], *pick[1:])

        pl.when(t == 0)(lambda: form_cross(24, 32))
        waiter(*field).wait_recv()
        field_a = hot_dot(pick_a[...], field_buf[t].reshape(IMG_ROW, LANES))
        spread(field_a, 0)
        from_a = products(0, weight_a)

        waiter(*pick).wait_recv()
        received = pick_buf[t].reshape(SLOTS, LANES)
        field_b = hot_dot(take_hot[...], received)
        spread(field_b, 1)
        from_b = products(1, weight_b)
        inner_next = fold(jnp.where(scalar_rows, received, 0.0))
        ratio = jnp.where(t == 0, 0.0, inner_next / inner_now)
        own = scaled + ratio * own
        dir_a = field_a + ratio * dir_a
        dir_b = field_b + ratio * dir_b
        prod_aa, prod_ca, prod_bb, prod_cb = prods
        prod_aa = from_a[:, 0:LANES] + ratio * prod_aa
        prod_ca = from_a[:, LANES:256] + ratio * prod_ca
        prod_bb = from_b + ratio * prod_bb
        step_row = total_of(
            fold(dir_a * prod_aa + dir_b * (2.0 * prod_ca + prod_bb)) + fold(damping * own * own)
        )
        sent = hot_dot(send_hot[...], prod_ca + prod_bb)
        prod_src[t] = jnp.where(scalar_rows, step_row, sent).reshape(N_COL, SLOT, LANES)
        prod_buf[t, col] = prod_src[t, col]
        send(prod[0], lambda peer: prod_src.at[t, peer], *prod[1:])

        prod_cb = products(1, weight_c) + ratio * prod_cb
        part = hot_dot(
            place_a[...],
            jnp.concatenate([prod_aa + prod_cb, jnp.zeros((LANES - BLOCKS, LANES), F32)], axis=0),
        )
        part_a_src[t] = part.reshape(N_COL, IMG, LANES)
        part_a_buf[t, col] = part_a_src[t, col]
        send(part_a[0], lambda peer: part_a_src.at[t, peer], *part_a[1:])

        waiter(*prod).wait_recv()
        received = prod_buf[t].reshape(SLOTS, LANES)
        part = hot_dot(place_b[...], received)
        part_b_src[t, :, 0:IMG, :] = part.reshape(N_ROW, IMG, LANES)
        step_row = fold(jnp.where(scalar_rows, received, 0.0))
        part_b_src[t, :, IMG : IMG + 1, :] = jnp.broadcast_to(step_row, (N_ROW, 1, LANES))
        part_b_buf[t, row] = part_b_src[t, row]
        send(part_b[0], lambda peer: part_b_src.at[t, peer], *part_b[1:])

        waiter(*part_a).wait_recv()
        image = damping * own + jnp.sum(part_a_buf[t], axis=0)
        for sent in (near, field, pick, prod, part_a):
            waiter(*sent).wait_send()
        waiter(*part_b).wait_recv()
        sums = jnp.sum(part_b_buf[t, :, 0 : IMG + 1, :], axis=0)
        image = image + sums[0:IMG]
        step_length = inner_next / sums[IMG : IMG + 1]
        for i, value in enumerate([update, own, residual, image]):
            vector_ref[i] = value
        for i, value in enumerate([dir_a, dir_b, prod_aa, prod_ca, prod_bb, prod_cb]):
            rows_state[i] = value
        scalar_ref[0] = jnp.broadcast_to(step_length, (8, LANES))
        scalar_ref[1] = jnp.broadcast_to(inner_next, (8, LANES))
        return carry

    vector_ref[...] = jnp.zeros_like(vector_ref)
    vector_ref[2] = right_side
    rows_state[...] = jnp.zeros_like(rows_state)
    scalar_ref[0] = jnp.zeros((8, LANES), F32)
    scalar_ref[1] = jnp.ones((8, LANES), F32)
    lax.fori_loop(0, ITERS, iteration, 0)
    state_ref[0:4] = vector_ref[...]
    state_ref[4] = jnp.broadcast_to(scalar_ref[0, 0:1, :], (IMG, LANES))

    waiter(3, rhs_r_buf, False, IMG).wait_send()

    def drain(t, carry):
        waiter(*exchanges(t)[-1]).wait_send()
        return carry

    lax.fori_loop(0, ITERS, drain, 0)


def shards(
    obs_jac,
    rad_jac,
    obs_residual,
    track_damping,
    track_block_column,
    track_slot,
    pair_rows,
    pair_cols,
    image_damping,
):

    def both(*shape, dtype=F32):
        return [pltpu.VMEM(shape, dtype)] * 2

    scratch = [
        pltpu.VMEM(obs_jac.shape, BF16),
        pltpu.VMEM(rad_jac.shape, F32),
        pltpu.VMEM(obs_residual.shape, F32),
        pltpu.VMEM(track_damping.shape, F32),
        pltpu.VMEM((BLOCKS * LANES, 256), BF16),
        *both(BLOCKS * LANES, LANES, dtype=BF16),
        pltpu.VMEM((BLOCKS, LANES, TRACKS), BF16),
        *both(BLOCKS, 256),
        *both(N_COL, SLOT, LANES),
        *both(N_COL, SLOT, 256),
        *both(N_COL, IMG, 256),
        *both(N_ROW, IMG, 256),
        pltpu.VMEM((ITERS, IMG + 8, LANES), F32),
        pltpu.VMEM((ITERS, N_ROW, IMG + 8, LANES), F32),
        pltpu.VMEM((ITERS, IMG, LANES), F32),
        pltpu.VMEM((ITERS, N_COL, IMG, LANES), F32),
        *both(ITERS, N_COL, SLOT, LANES),
        *both(ITERS, N_COL, SLOT, LANES),
        *both(ITERS, N_COL, IMG, LANES),
        *both(ITERS, N_ROW, IMG + 8, LANES),
        pltpu.VMEM((2, 2 * BLOCKS, BLOCKS * LANES), BF16),
        pltpu.VMEM((SLOTS, BLOCKS), BF16),
        pltpu.VMEM((BLOCKS, SLOTS), BF16),
        pltpu.VMEM((BLOCKS, IMG_ROW), BF16),
        pltpu.VMEM((IMG_ROW, LANES), BF16),
        *both(SLOTS, LANES, dtype=BF16),
        pltpu.VMEM((4, IMG, LANES), F32),
        pltpu.VMEM((6, BLOCKS, LANES), F32),
        pltpu.VMEM((2, 8, LANES), F32),
        pltpu.SemaphoreType.DMA((3,)),
        pltpu.SemaphoreType.DMA((BLOCKS // STEP,)),
        pltpu.SemaphoreType.DMA((PHASES,)),
        pltpu.SemaphoreType.DMA((PHASES,)),
    ]
    hbm = pl.BlockSpec(memory_space=pltpu.HBM)
    vmem = pl.BlockSpec(memory_space=pltpu.VMEM)
    state = (
        pl.pallas_call(
            kernel,
            out_shape=jax.ShapeDtypeStruct((5, IMG, LANES), F32),
            in_specs=[hbm] * 4 + [vmem] * 5,
            out_specs=vmem,
            scratch_shapes=scratch,
            compiler_params=pltpu.CompilerParams(
                collective_id=0, has_side_effects=True, vmem_limit_bytes=56 * 1024 * 1024
            ),
        )(
            obs_jac,
            rad_jac,
            obs_residual,
            track_damping,
            image_damping,
            track_block_column.reshape(1, BLOCKS),
            track_slot.reshape(1, BLOCKS),
            pair_rows.reshape(1, BLOCKS),
            pair_cols.reshape(1, BLOCKS),
        )
    )
    return state[0] + state[4] * state[1], state[2] - state[4] * state[3]


def solution(mesh):
    in_specs = (
        P(("row", "col"), None, None, None),
        P(("row", "col"), None, None),
        P(("row", "col"), None, None),
        P(("row", "col"), None),
        P(("row", "col"), None),
        P(("row", "col")),
        P(("row", "col")),
        P(("row", "col")),
        P(("row", "col"), None),
    )
    out_specs = (P(("row", "col"), None), P(("row", "col"), None))
    return jax.shard_map(shards, mesh=mesh, in_specs=in_specs, out_specs=out_specs, check_vma=False)
```
